32 devices in a mesh: ctx: 8 (over z, y), ch: 4 (over x, core).
Axes of the slice: x: 2, y: 2, z: 4, core: 2. Of those that a mesh axis runs over, the one named last changes fastest.
Arguments:
- signal: bfloat16 [256, 512, 1024], P('ctx', None, 'ch'), may hold values from -15 to 15
- factor_first: bfloat16 [4, 512, 512], P('ch'), may hold values from -0.25 to 0.25
- factor_second: bfloat16 [4, 256, 256], P('ch'), may hold values from -0.375 to 0.375
- up_weight: bfloat16 [4, 256, 1024], P('ch'), may hold values from -0.375 to 0.375
- down_weight: bfloat16 [4, 1024, 256], P('ch'), may hold values from -0.1875 to 0.1875
- norm_gain: float32 [4, 256], P('ch'), may hold values from 0.1 to 1.9
- cotangent: bfloat16 [512, 256, 1024], P('ctx', None, 'ch'), may hold values from -6 to 6
Outputs:
- layer_out: bfloat16 [512, 256, 1024], P('ctx', None, 'ch')
- grad_signal: bfloat16 [256, 512, 1024], P('ctx', None, 'ch')
- grad_first: float32 [4, 512, 512], P('ch', 'ctx')
- grad_second: float32 [4, 256, 256], P('ch', 'ctx')
- grad_up: float32 [4, 256, 1024], P('ch', 'ctx')
- grad_down: float32 [4, 1024, 256], P('ch', 'ctx')
- grad_gain: float32 [4, 256], P('ch', 'ctx')
The draws below stay inside these ranges and needn't reach their ends.
All inputs are finite; a program needn't handle non-finite values.
Results may differ from the reference program's by a relative error of at most 0.0095.
Values may be sent and summed in bfloat16 or wider, within the bound.
No kernel may reach another device: no remote copies, remote signals or barrier semaphores. Data moves between devices by JAX's collectives and lax.ppermute only.
A program may use at most 256 MiB of HBM per device.

```python
import math
import jax
import jax.numpy as jnp
from jax import lax

D = 1024
G = 4
DG = 256
HG = 1024
NB = 512
NA = 256


def draw_signal(key, part):
    noise_key, scale_key = jax.random.split(key)
    channel_ramp = jnp.arange(D, dtype=jnp.float32) / (D - 1)
    values = jax.random.truncated_normal(noise_key, -4.0, 4.0, (NA, NB, D), jnp.float32)
    spread = jax.random.uniform(scale_key, (D,), jnp.float32, 0.0, math.log(4.0))
    scales = 0.3 * jnp.exp(spread + channel_ramp * math.log(3.0))
    return (values * scales).astype(jnp.bfloat16)


def levels(stream_key, extent, cuts, least, high):
    loudness, own = 1.0, jax.random.fold_in(stream_key, 6)
    for axis_at, blocks in cuts:
        draws = jnp.exp(jax.random.uniform(jax.random.fold_in(own, axis_at), (blocks,), jnp.float32, least / len(cuts), high / len(cuts)))
        loudness = loudness * jnp.repeat(draws, extent[axis_at] // blocks).reshape([-1 if axis == axis_at else 1 for axis in range(len(extent))])
    return loudness


def noise(stream_key, dims, width, most, pieces=(), kind=jnp.bfloat16):
    entries = width * jax.random.normal(stream_key, dims, jnp.float32)
    if pieces:
        entries = entries * levels(stream_key, dims, pieces, -0.22, 0.18)
    return jnp.clip(entries, -most, most).astype(kind)


def setup_inputs(seed: int = 0) -> dict:
    key_of = jax.random.split(jax.random.key(seed), 8)
    signal = draw_signal(jax.random.fold_in(key_of[7], 71), 0)
    factor_first = noise(key_of[1], (G, NB, NB), NB ** -0.5, 0.25, ((0, 4),))
    factor_second = noise(key_of[2], (G, NA, NA), NA ** -0.5, 0.375, ((0, 4),))
    up_weight = noise(key_of[3], (G, DG, HG), DG ** -0.5, 0.375, ((0, 4),))
    down_weight = noise(key_of[4], (G, HG, DG), HG ** -0.5, 0.1875, ((0, 4),))
    norm_gain = jnp.clip(1.0 + 0.18 * jax.random.normal(key_of[5], (G, DG), jnp.float32), 0.1, 1.9)
    cotangent = noise(key_of[6], (NB, NA, D), 1.0, 6.0, ((0, 8), (2, 4)))
    return dict(signal=signal, factor_first=factor_first, factor_second=factor_second, up_weight=up_weight, down_weight=down_weight, norm_gain=norm_gain, cotangent=cotangent)


EPSILON = 1e-05

def group_mix(inputs, first_block, second_block):
    values = inputs.astype(jnp.float32)
    first_mix = jnp.einsum('abc,bj->ajc', values, first_block.astype(jnp.float32))
    gate_open = jax.nn.sigmoid(values)
    gated_rows = (first_mix * gate_open).astype(jnp.bfloat16)
    mixed_rows = jnp.einsum('ajc,ai->jic', gated_rows.astype(jnp.float32), second_block.astype(jnp.float32))
    return (first_mix, gate_open, gated_rows, mixed_rows)

def reference(signal, factor_first, factor_second, up_weight, down_weight, norm_gain, cotangent):
    group_width = D // G
    by_group = signal.reshape(NA, NB, G, group_width).transpose(2, 0, 1, 3)
    upstream = cotangent.reshape(NB, NA, G, group_width).transpose(2, 0, 1, 3)
    mixed_all = lax.map(lambda parts: group_mix(parts[0], parts[1], parts[2])[3], (by_group, factor_first, factor_second))
    mean_square = lax.optimization_barrier(jnp.sum(mixed_all * mixed_all, axis=(0, 3))) / D
    inverse = lax.rsqrt(mean_square + EPSILON)[:, :, None]

    def mlp_group(parts):
        mixed_rows, gain_row, up_block, down_block, upstream_rows = parts
        gain_values = gain_row.astype(jnp.float32)
        normed = (mixed_rows * inverse * gain_values).astype(jnp.bfloat16)
        preact = jnp.einsum('jic,ch->jih', normed.astype(jnp.float32), up_block.astype(jnp.float32))
        activation, gelu_back = jax.vjp(jax.nn.gelu, preact)
        act_rows = activation.astype(jnp.bfloat16)
        down_float = down_block.astype(jnp.float32)
        layer_rows = (mixed_rows + jnp.einsum('jih,hc->jic', act_rows.astype(jnp.float32), down_float)).astype(jnp.bfloat16)
        upstream_float = upstream_rows.astype(jnp.float32)
        grad_act = jnp.einsum('jic,hc->jih', upstream_float, down_float)
        grad_pre = gelu_back(grad_act)[0].astype(jnp.bfloat16)
        grad_down = jnp.einsum('jih,jic->hc', act_rows.astype(jnp.float32), upstream_float)
        grad_up = jnp.einsum('jic,jih->ch', normed.astype(jnp.float32), grad_pre.astype(jnp.float32))
        grad_normed = jnp.einsum('jih,ch->jic', grad_pre.astype(jnp.float32), up_block.astype(jnp.float32))
        grad_gain = lax.optimization_barrier(jnp.sum(grad_normed * mixed_rows * inverse, axis=(0, 1)))
        grad_scaled = grad_normed * gain_values
        cross_part = lax.optimization_barrier(jnp.sum(grad_scaled * mixed_rows, axis=2))
        return (layer_rows, grad_down, grad_up, grad_gain, grad_scaled, cross_part)
    layer_groups, grad_downs, grad_ups, grad_gains, scaled_all, cross_parts = lax.map(mlp_group, (mixed_all, norm_gain, up_weight, down_weight, upstream))
    cross = lax.optimization_barrier(jnp.sum(cross_parts, axis=0)) / D

    def back_group(parts):
        inputs, first_block, second_block, mixed_rows, grad_scaled, upstream_rows = parts
        first_mix, gate_open, gated_rows, unused = group_mix(inputs, first_block, second_block)
        grad_mixed = (upstream_rows.astype(jnp.float32) + inverse * grad_scaled - inverse ** 3 * mixed_rows * cross[:, :, None]).astype(jnp.bfloat16)
        grad_second = jnp.einsum('ajc,jic->ai', gated_rows.astype(jnp.float32), grad_mixed.astype(jnp.float32))
        grad_gated = jnp.einsum('jic,ai->ajc', grad_mixed.astype(jnp.float32), second_block.astype(jnp.float32)).astype(jnp.bfloat16)
        gated_float = grad_gated.astype(jnp.float32)
        grad_first_mix = (gated_float * gate_open).astype(jnp.bfloat16)
        grad_gate = gated_float * first_mix * gate_open * (1.0 - gate_open)
        grad_input = (jnp.einsum('ajc,bj->abc', grad_first_mix.astype(jnp.float32), first_block.astype(jnp.float32)) + grad_gate).astype(jnp.bfloat16)
        grad_first = jnp.einsum('abc,ajc->bj', inputs.astype(jnp.float32), grad_first_mix.astype(jnp.float32))
        return (grad_input, grad_first, grad_second)
    grad_inputs, grad_firsts, grad_seconds = lax.map(back_group, (by_group, factor_first, factor_second, mixed_all, scaled_all, upstream))
    grad_scale = (NA * NB) ** (-0.5)
    layer_out = layer_groups.transpose(1, 2, 0, 3).reshape(NB, NA, D)
    grad_signal = grad_inputs.transpose(1, 2, 0, 3).reshape(NA, NB, D)
    return (layer_out, grad_signal, grad_firsts * grad_scale, grad_seconds * grad_scale, grad_ups * grad_scale, grad_downs * grad_scale, grad_gains * grad_scale)
```

```python
import functools

import jax
import jax.numpy as jnp
from jax import lax
from jax.experimental import pallas as pl
from jax.experimental.pallas import tpu as pltpu
from jax.sharding import PartitionSpec as P

EPSILON = 1e-05
TANH_SCALE = 0.7978845608028654
TANH_CUBIC = 0.044715
BF16 = jnp.bfloat16
F32 = jnp.float32
VMEM_LIMIT = 56 * 1024 * 1024


def sigmoid(values):
    return 0.5 * jnp.tanh(0.5 * values) + 0.5


def dot(left, right, left_dim, right_dim):
    return lax.dot_general(
        left, right, (((left_dim,), (right_dim,)), ((), ())), preferred_element_type=F32
    )


def to_row(column):
    return jnp.broadcast_to(column, (column.shape[0], 128)).T[0:1, :]


def to_column(row, width):
    spread = jnp.broadcast_to(row, (128, row.shape[1])).T
    return jnp.concatenate([spread] * (width // 128), axis=1)


def call(body, out_shape, cost, operands, in_specs, after=(), **options):
    flops, bytes_accessed = cost
    given, waits = len(operands), len(after)

    def ordered(*refs):
        body(*refs[:given], *refs[given + waits :])

    return pl.pallas_call(
        ordered,
        out_shape=out_shape,
        in_specs=[*in_specs, *([pl.BlockSpec(memory_space=pl.ANY)] * waits)],
        compiler_params=pltpu.CompilerParams(vmem_limit_bytes=VMEM_LIMIT),
        cost_estimate=pl.CostEstimate(
            flops=int(flops), bytes_accessed=int(bytes_accessed), transcendentals=0
        ),
        **options,
    )(*operands, *after)


def whole(array):
    return pl.BlockSpec(array.shape, lambda s: (0,) * array.ndim)


def first_mix_body(slab, offset, ctx, signal_ref, factor_ref, gated_ref, slope_ref, turn):
    rows, depth, width = signal_ref.shape
    piece = gated_ref.shape[0] // ctx
    count = ctx * piece
    for a in range(rows):
        first = dot(factor_ref[...], signal_ref[a], 1, 0)
        own = jnp.concatenate(
            [signal_ref[a, d * slab + offset : d * slab + offset + piece, :] for d in range(ctx)],
            axis=0,
        )
        gate = sigmoid(own.astype(F32))
        gated = first * gate
        slope_ref[a] = (gated * (1.0 - gate)).astype(BF16)
        for lane in range(width // 128):
            turn[lane, pl.ds(a, count, stride=rows), :] = gated[:, lane * 128 : (lane + 1) * 128]
    for lane in range(width // 128):
        gated_ref[:, :, lane * 128 : (lane + 1) * 128] = (
            turn[lane].reshape(count, rows, 128).astype(BF16)
        )


def first_mix(signal, factor_turned, slab, offset, ctx, after=()):
    rows, depth, width = signal.shape
    count = factor_turned.shape[0]
    block = min(16, rows)
    return call(
        functools.partial(first_mix_body, slab, offset, ctx),
        (
            jax.ShapeDtypeStruct((count, rows, width), BF16),
            jax.ShapeDtypeStruct((rows, count, width), BF16),
        ),
        (2 * rows * depth * count * width, 2 * rows * width * (depth + 2 * count)),
        (signal, factor_turned),
        [
            pl.BlockSpec((block, depth, width), lambda s: (s, 0, 0)),
            pl.BlockSpec((count, depth), lambda s: (0, 0)),
        ],
        after,
        grid=(rows // block,),
        out_specs=(
            pl.BlockSpec((count, block, width), lambda s: (0, s, 0)),
            pl.BlockSpec((block, count, width), lambda s: (s, 0, 0)),
        ),
        scratch_shapes=[pltpu.VMEM((width // 128, count * block, 128), F32)],
        name="first_mix",
    )


def tokens_of(gated_ref, t):
    ctx, _, rows, width = gated_ref.shape
    return gated_ref[:, t].reshape(ctx * rows, width)


def square_body(gated_ref, factor_ref, square_ref):
    steps, inner, _ = square_ref.shape
    for t in range(steps * inner):
        mixed = dot(factor_ref[...], tokens_of(gated_ref, t), 1, 0)
        square_ref[t // inner, t % inner : t % inner + 1, :] = to_row(
            jnp.sum(mixed * mixed, axis=1, keepdims=True)
        )


def squares(gated, factor_turned, inner, after=()):
    ctx, piece, rows, width = gated.shape
    tall = factor_turned.shape[0]
    block = min(8, piece)
    return call(
        square_body,
        jax.ShapeDtypeStruct((piece // inner, inner, tall), F32),
        (2 * piece * tall * tall * width, 2 * gated.size),
        (gated, factor_turned),
        [
            pl.BlockSpec((ctx, block, rows, width), lambda s: (0, s, 0, 0)),
            whole(factor_turned),
        ],
        after,
        grid=(piece // block,),
        out_specs=pl.BlockSpec((block // inner, inner, tall), lambda s: (s, 0, 0)),
        name="squares",
    )


def gathered(parts_ref, step, t):
    return sum(parts_ref[g, step, t : t + 1, :] for g in range(parts_ref.shape[0]))


def inverse_of(square_ref, step, t, channels):
    return lax.rsqrt(gathered(square_ref, step, t) * (1.0 / channels) + EPSILON)


def mlp_body(
    channels, carried, gated_ref, factor_ref, square_ref, gain_ref, up_ref, up_turned_ref,
    down_ref, down_turned_ref, cotangent_ref, up_in_ref, down_in_ref, gain_in_ref, *refs,
):
    (layer_ref, pull_ref, cross_ref, up_out_ref, down_out_ref, gain_out_ref,
     mixed_all, normed_all, act_all, pre_all, spread_all) = refs[carried:]
    inner = square_ref.shape[2]
    tall = factor_ref.shape[0]
    width = gain_ref.shape[1]
    hidden = up_ref.shape[1]

    @pl.when(pl.program_id(0) == 0)
    def _():
        up_out_ref[...] = up_in_ref[...]
        down_out_ref[...] = down_in_ref[...]
        gain_out_ref[...] = gain_in_ref[...]

    for t in range(inner):
        inverse = inverse_of(square_ref, 0, t, channels)
        part = slice(t * tall, (t + 1) * tall)
        mixed = dot(factor_ref[...], tokens_of(gated_ref, t), 1, 0)
        spread = to_column(inverse, width)
        mixed_all[part, :] = mixed
        spread_all[part, :] = spread
        normed_all[part, :] = (mixed * spread * gain_ref[...]).astype(BF16)
    upstream = cotangent_ref[...].reshape(inner * tall, width)
    normed = normed_all[...]
    step = min(256, hidden)
    for h in range(0, hidden, step):
        part = slice(h, h + step)
        pre = dot(normed, up_ref[:, part], 1, 0)
        back = dot(upstream, down_turned_ref[:, part], 1, 0)
        square = pre * pre
        lean = jnp.tanh(pre * (square * (TANH_SCALE * TANH_CUBIC) + TANH_SCALE))
        half = 0.5 * lean + 0.5
        act = pre * half
        act_all[:, part] = act.astype(BF16)
        bend = square * (6.0 * TANH_SCALE * TANH_CUBIC) + 2.0 * TANH_SCALE
        pre_all[:, part] = (back * (half + act * (1.0 - half) * bend)).astype(BF16)
    mixed = mixed_all[...]
    layer = mixed + dot(act_all[...], down_ref[...], 1, 0)
    layer_ref[...] = layer.astype(BF16).reshape(layer_ref.shape)
    down_out_ref[...] += dot(upstream, act_all[...], 0, 0)
    up_out_ref[...] += dot(normed, pre_all[...], 0, 0)
    grad_normed = dot(pre_all[...], up_turned_ref[...], 1, 0)
    spread = spread_all[...]
    gain = gain_ref[...]
    weighed = grad_normed * mixed
    gain_out_ref[...] += jnp.sum(weighed * spread, axis=0, keepdims=True)
    cross = jnp.sum(weighed * gain, axis=1, keepdims=True)
    for t in range(inner):
        cross_ref[0, t : t + 1, :] = to_row(cross[t * tall : (t + 1) * tall])
    pull_ref[...] = (grad_normed * gain * spread).astype(BF16).reshape(pull_ref.shape)


def mlp(gated, part, factor_turned, square, gain, up, up_turned, down, down_turned, cotangent,
        first_piece, sums, layer_pull, channels, after=()):
    ctx, _, rows, width = gated.shape
    groups, _, inner, tall = square.shape
    hidden = up.shape[1]
    begin, piece = part
    steps, skip = piece // inner, begin // inner
    start = (first_piece + begin) // inner
    tokens = inner * tall
    by_token = pl.BlockSpec((inner, tall, width), lambda s: (s + start, 0, 0))
    stays = pl.BlockSpec(memory_space=pl.ANY)
    full = jax.ShapeDtypeStruct(cotangent.shape, BF16)
    carried = len(layer_pull)
    aliases = {9: 3, 10: 4, 11: 5}
    for i in range(carried):
        aliases[12 + i] = i
    return call(
        functools.partial(mlp_body, channels, carried),
        (
            full,
            full,
            jax.ShapeDtypeStruct((steps, inner, tall), F32),
            *(jax.ShapeDtypeStruct(array.shape, F32) for array in sums),
        ),
        (12 * piece * tall * width * hidden, 8 * piece * tall * width),
        (gated, factor_turned, square, gain, up, up_turned, down, down_turned, cotangent, *sums,
         *layer_pull),
        [
            pl.BlockSpec((ctx, inner, rows, width), lambda s: (0, s + skip, 0, 0)),
            whole(factor_turned),
            pl.BlockSpec((groups, 1, inner, tall), lambda s: (0, s + skip, 0, 0)),
            whole(gain), whole(up), whole(up_turned), whole(down), whole(down_turned),
            by_token,
            *(whole(array) for array in sums),
            *([stays] * carried),
        ],
        after,
        grid=(steps,),
        out_specs=(
            by_token, by_token,
            pl.BlockSpec((1, inner, tall), lambda s: (s, 0, 0)),
            *(whole(array) for array in sums),
        ),
        scratch_shapes=[
            pltpu.VMEM((tokens, width), F32),
            pltpu.VMEM((tokens, width), BF16),
            pltpu.VMEM((tokens, hidden), BF16),
            pltpu.VMEM((tokens, hidden), BF16),
            pltpu.VMEM((tokens, width), F32),
        ],
        input_output_aliases=aliases,
        name="mlp",
    )


def second_body(
    channels, gated_ref, factor_ref, factor_turned_ref, square_ref, cross_ref, pull_ref,
    cotangent_ref, sum_in_ref, moved_ref, sum_out_ref,
):
    _, steps, inner, tall = square_ref.shape
    ctx, _, rows, width = gated_ref.shape

    @pl.when(pl.program_id(0) == 0)
    def _():
        sum_out_ref[...] = sum_in_ref[...]

    total = sum_out_ref[...]
    for t in range(steps * inner):
        gated = tokens_of(gated_ref, t)
        mixed = dot(factor_turned_ref[...], gated, 1, 0)
        inverse = inverse_of(square_ref, t // inner, t % inner, channels)
        cross = gathered(cross_ref, t // inner, t % inner)
        weight = to_column(inverse * inverse * inverse * cross * (1.0 / channels), width)
        grad = (
            cotangent_ref[t].astype(F32) + pull_ref[t].astype(F32) - mixed * weight
        ).astype(BF16)
        total += dot(gated, grad, 1, 1)
        moved_ref[:, t] = dot(factor_ref[...], grad, 1, 0).astype(BF16).reshape(ctx, rows, width)
    sum_out_ref[...] = total


def second(gated, factor, factor_turned, square, cross, pull, cotangent, first_piece, total,
           channels, after=()):
    ctx, piece, rows, width = gated.shape
    groups, steps, inner, tall = square.shape
    block = max(size for size in (4, 2, 1) if steps % size == 0)
    count = block * inner
    start = first_piece // count
    by_piece = pl.BlockSpec((groups, block, inner, tall), lambda s: (0, s, 0, 0))
    by_token = pl.BlockSpec((count, tall, width), lambda s: (s + start, 0, 0))
    return call(
        functools.partial(second_body, channels),
        (
            jax.ShapeDtypeStruct(gated.shape, BF16),
            jax.ShapeDtypeStruct(total.shape, F32),
        ),
        (6 * piece * tall * tall * width, 8 * gated.size),
        (gated, factor, factor_turned, square, cross, pull, cotangent, total),
        [
            pl.BlockSpec((ctx, count, rows, width), lambda s: (0, s, 0, 0)),
            whole(factor), whole(factor_turned), by_piece, by_piece, by_token, by_token,
            whole(total),
        ],
        after,
        grid=(steps // block,),
        out_specs=(
            pl.BlockSpec((ctx, count, rows, width), lambda s: (0, s, 0, 0)),
            whole(total),
        ),
        input_output_aliases={7: 1},
        name="second",
    )


def gate_body(slab, offset, ctx, moved_ref, signal_ref, slope_ref, first_ref, gate_ref, sum_ref,
              turn):
    rows, depth, width = signal_ref.shape
    count = moved_ref.shape[0]
    piece = count // ctx

    @pl.when(pl.program_id(0) == 0)
    def _():
        sum_ref[...] = jnp.zeros_like(sum_ref)

    for lane in range(width // 128):
        turn[lane] = (
            moved_ref[:, :, lane * 128 : (lane + 1) * 128]
            .astype(F32)
            .reshape(count * rows, 128)
        )
    total = sum_ref[...]
    for a in range(rows):
        grad = jnp.concatenate(
            [turn[lane, pl.ds(a, count, stride=rows), :] for lane in range(width // 128)], axis=1
        )
        own = jnp.concatenate(
            [signal_ref[a, d * slab + offset : d * slab + offset + piece, :] for d in range(ctx)],
            axis=0,
        )
        first = (grad * sigmoid(own.astype(F32))).astype(BF16)
        first_ref[a] = first
        gate_ref[a] = (grad * slope_ref[a].astype(F32)).astype(BF16)
        total += dot(signal_ref[a], first, 1, 1)
    sum_ref[...] = total


def gate(moved, signal, slope, slab, offset, ctx, after=()):
    rows, depth, width = signal.shape
    count = moved.shape[0]
    block = min(16, rows)
    by_row = pl.BlockSpec((block, count, width), lambda s: (s, 0, 0))
    return call(
        functools.partial(gate_body, slab, offset, ctx),
        (
            jax.ShapeDtypeStruct((rows, count, width), BF16),
            jax.ShapeDtypeStruct((rows, count, width), BF16),
            jax.ShapeDtypeStruct((depth, count), F32),
        ),
        (2 * rows * depth * count * width, 2 * rows * width * (depth + 4 * count)),
        (moved, signal, slope),
        [
            pl.BlockSpec((count, block, width), lambda s: (0, s, 0)),
            pl.BlockSpec((block, depth, width), lambda s: (s, 0, 0)),
            by_row,
        ],
        after,
        grid=(rows // block,),
        out_specs=(by_row, by_row, pl.BlockSpec((depth, count), lambda s: (0, 0))),
        scratch_shapes=[pltpu.VMEM((width // 128, count * block, 128), F32)],
        name="gate",
    )


def signal_body(offsets, slab, ctx, factor_ref, *refs):
    pieces = len(offsets)
    firsts, gates, out_ref = refs[:pieces], refs[pieces : 2 * pieces], refs[-1]
    for a in range(out_ref.shape[0]):
        grads = jnp.concatenate([first[a] for first in firsts], axis=0)
        total = dot(factor_ref[...], grads, 1, 0)
        for gate_ref, offset in zip(gates, offsets):
            piece = gate_ref.shape[1] // ctx
            for d in range(ctx):
                place = slice(d * slab + offset, d * slab + offset + piece)
                out_ref[a, place, :] = (
                    total[place] + gate_ref[a, d * piece : (d + 1) * piece, :].astype(F32)
                ).astype(BF16)


def signal_grad(factor, firsts, gates, offsets, slab, ctx, after=()):
    rows, _, width = firsts[0].shape
    depth = factor.shape[0]
    block = min(4, rows)
    by_row = [pl.BlockSpec((block, *array.shape[1:]), lambda s: (s, 0, 0)) for array in firsts]
    return call(
        functools.partial(signal_body, offsets, slab, ctx),
        jax.ShapeDtypeStruct((rows, depth, width), BF16),
        (2 * rows * depth * depth * width, 6 * rows * depth * width),
        (factor, *firsts, *gates),
        [whole(factor), *by_row, *by_row],
        after,
        grid=(rows // block,),
        out_specs=pl.BlockSpec((block, depth, width), lambda s: (s, 0, 0)),
        name="signal_grad",
    )


def scatter_total(partial_sum, ctx):
    if ctx & (ctx - 1):
        return lax.psum_scatter(partial_sum, "ctx", scatter_dimension=0, tiled=False)
    me = lax.axis_index("ctx")
    bit = 1
    values = partial_sum
    while bit < ctx:
        halves = values.reshape((-1, 2) + values.shape[1:])
        mine = (me // bit) % 2
        keep = lax.dynamic_index_in_dim(halves, mine, 1, keepdims=False)
        give = lax.dynamic_index_in_dim(halves, 1 - mine, 1, keepdims=False)
        got = lax.ppermute(give.astype(BF16), "ctx", [(i, i ^ bit) for i in range(ctx)])
        values = keep + got.astype(F32)
        bit *= 2
    return values[0]


def block_total_body(parts_ref, total_ref):
    total_ref[...] = jnp.sum(parts_ref[...].astype(F32), axis=0)


def block_total(parts, after=()):
    return call(
        block_total_body,
        jax.ShapeDtypeStruct(parts.shape[1:], F32),
        (parts.size, 4 * parts.size),
        (parts,),
        [whole(parts)],
        after,
        grid=(1,),
        out_specs=pl.BlockSpec(parts.shape[1:], lambda s: (0, 0)),
        name="block_total",
    )


def from_groups(partial_value):
    return lax.all_gather(partial_value, "ch")


def exchange(block):
    return lax.all_to_all(block, "ctx", split_axis=0, concat_axis=0, tiled=True)


def shards(ctx, channels, token_count, signal, factor_first, factor_second, up_weight,
           down_weight, norm_gain, cotangent):
    rows, depth, width = signal.shape
    slab, tall, _ = cotangent.shape
    first, factor = factor_first[0], factor_second[0]
    up, down = up_weight[0], down_weight[0]
    hidden = up.shape[1]
    factor_turned, up_turned, down_turned = factor.T, up.T, down.T
    unit = min(16, slab)
    sizes = (unit, slab - 2 * unit, unit) if slab > 2 * unit else (slab,)
    last = len(sizes) - 1
    offsets = tuple(sum(sizes[:k]) for k in range(len(sizes)))
    inner = 2
    by_owner = first.reshape(depth, ctx, slab)
    columns = [
        by_owner[:, :, start : start + size].reshape(depth, ctx * size)
        for start, size in zip(offsets, sizes)
    ]
    mix = lambda k, after=(): first_mix(signal, columns[k].T, slab, offsets[k], ctx, after)
    sent = lambda k, gated: exchange(gated).reshape(ctx, sizes[k], rows, width)
    total = len(sizes)
    slopes, arrived, squared, crossed, moved = ([None] * total for _ in range(5))
    sums = (
        jnp.zeros((width, hidden), F32),
        jnp.zeros((width, hidden), F32),
        jnp.zeros((1, width), F32),
    )
    state = dict(sums=sums, layer_pull=(), second=jnp.zeros((tall, tall), F32))

    def square_of(k, after=()):
        squared[k] = from_groups(squares(arrived[k], factor_turned, inner, after))

    def mlp_of(k, begin, size, after=()):
        layer, pull, cross, *new_sums = mlp(
            arrived[k], (begin, size), factor_turned, squared[k], norm_gain, up, up_turned, down,
            down_turned, cotangent, offsets[k], state["sums"], state["layer_pull"], channels,
            after,
        )
        state.update(sums=new_sums, layer_pull=(layer, pull))
        return cross

    def second_of(k, after=()):
        out, state["second"] = second(
            arrived[k], factor, factor_turned, squared[k], crossed[k], state["layer_pull"][1],
            cotangent, offsets[k], state["second"], channels, after,
        )
        moved[k] = out.reshape(ctx * sizes[k], rows, width)
        return out

    def back(k):
        moved[k] = exchange(moved[k])

    def gate_of(k, after=()):
        return gate(moved[k], signal, slopes[k], slab, offsets[k], ctx, after)

    first_block = lambda sums: sums.reshape(ctx, depth // ctx, sums.shape[1])
    outs = [None] * total
    gated, slopes[0] = mix(0)
    arrived[0] = sent(0, gated)
    if last:
        gated, slopes[1] = mix(1)
        arrived[1] = sent(1, gated)
        square_of(0)
        cross_0 = mlp_of(0, 0, sizes[0])
        gated, slopes[2] = mix(2, (cross_0,))
        arrived[2] = sent(2, gated)
        crossed[0] = from_groups(cross_0)
        square_of(1, (cross_0,))
        cross_1 = mlp_of(1, 0, unit)
        done = second_of(0, (cross_1,))
        back(0)
        cross_2 = mlp_of(1, unit, sizes[1] - unit, (done,))
        crossed[1] = from_groups(jnp.concatenate([cross_1, cross_2]))
        done = second_of(1)
        back(1)
        square_of(2, (done, moved[0]))
        crossed[2] = from_groups(mlp_of(2, 0, sizes[2]))
        done = second_of(2)
        back(2)
    else:
        square_of(0)
        crossed[0] = from_groups(mlp_of(0, 0, sizes[0]))
        done = second_of(0)
        back(0)
    for k in range(total):
        outs[k] = gate_of(k)
    first_sums = [
        scatter_total(first_block(out[2]), ctx).reshape(depth // ctx, ctx, size)
        for out, size in zip(outs[:-1], sizes)
    ]
    parts = exchange(outs[-1][2].astype(BF16)).reshape(ctx, depth // ctx, ctx * sizes[-1])
    grad_signal = signal_grad(
        jnp.concatenate(columns, axis=1),
        [out[0] for out in outs], [out[1] for out in outs], offsets, slab, ctx,
    )
    first_sums.append(
        block_total(parts, (grad_signal,)).reshape(depth // ctx, ctx, sizes[-1])
    )
    scale = token_count ** (-0.5)
    grad_first = jnp.concatenate(first_sums, axis=2).reshape(1, depth // ctx, depth)
    up_sum, down_sum, gain_sum = state["sums"]
    packed = jnp.concatenate(
        [
            up_sum.reshape(ctx, width // ctx * (hidden // tall), tall),
            down_sum.T.reshape(ctx, hidden * width // (ctx * tall), tall),
            state["second"].reshape(ctx, tall // ctx, tall),
            jnp.broadcast_to(gain_sum.reshape(ctx, width // ctx, 1), (ctx, width // ctx, tall)),
        ],
        axis=1,
    )
    packed = scatter_total(packed, ctx) * scale
    ends = (width // ctx * (hidden // tall), hidden * width // (ctx * tall), tall // ctx)
    a, b, c = ends[0], ends[0] + ends[1], sum(ends)
    return (
        state["layer_pull"][0],
        grad_signal,
        grad_first * scale,
        packed[b:c][None],
        packed[:a].reshape(1, width // ctx, hidden),
        packed[a:b].reshape(1, hidden // ctx, width),
        packed[c:, 0][None],
    )


def solution(mesh):
    placed = (
        P("ctx", None, "ch"),
        P("ch", None, None),
        P("ch", None, None),
        P("ch", None, None),
        P("ch", None, None),
        P("ch", None),
        P("ctx", None, "ch"),
    )

    def layer(signal, factor_first, factor_second, up_weight, down_weight, norm_gain, cotangent):
        body = functools.partial(
            shards, mesh.shape["ctx"], signal.shape[2], signal.shape[0] * signal.shape[1]
        )
        return jax.shard_map(
            body,
            mesh=mesh,
            in_specs=placed,
            out_specs=(
                P("ctx", None, "ch"),
                P("ctx", None, "ch"),
                P("ch", "ctx", None),
                P("ch", "ctx", None),
                P("ch", "ctx", None),
                P("ch", "ctx", None),
                P("ch", "ctx"),
            ),
            check_vma=False,
        )(signal, factor_first, factor_second, up_weight, down_weight, norm_gain, cotangent)

    return layer
```

```python
import functools

import jax
import jax.numpy as jnp
from jax import lax
from jax.experimental import pallas as pl
from jax.experimental.pallas import tpu as pltpu
from jax.sharding import PartitionSpec as P

EPSILON = 1e-05
TANH_SCALE = 0.7978845608028654
TANH_CUBIC = 0.044715
BF16 = jnp.bfloat16
F32 = jnp.float32
VMEM_LIMIT = 56 * 1024 * 1024


def sigmoid(values):
    return 0.5 * jnp.tanh(0.5 * values) + 0.5


def dot(left, right, left_dim, right_dim):
    return lax.dot_general(
        left, right, (((left_dim,), (right_dim,)), ((), ())), preferred_element_type=F32
    )


def to_row(column):
    return jnp.broadcast_to(column, (column.shape[0], 128)).T[0:1, :]


def to_column(row, width):
    spread = jnp.broadcast_to(row, (128, row.shape[1])).T
    return jnp.concatenate([spread] * (width // 128), axis=1)


def call(body, out_shape, cost, operands, in_specs, after=(), **options):
    flops, bytes_accessed = cost
    given, waits = len(operands), len(after)

    def ordered(*refs):
        body(*refs[:given], *refs[given + waits :])

    return pl.pallas_call(
        ordered,
        out_shape=out_shape,
        in_specs=[*in_specs, *([pl.BlockSpec(memory_space=pl.ANY)] * waits)],
        compiler_params=pltpu.CompilerParams(vmem_limit_bytes=VMEM_LIMIT),
        cost_estimate=pl.CostEstimate(
            flops=int(flops), bytes_accessed=int(bytes_accessed), transcendentals=0
        ),
        **options,
    )(*operands, *after)


def whole(array):
    return pl.BlockSpec(array.shape, lambda s: (0,) * array.ndim)


def first_mix_body(slab, offset, ctx, signal_ref, factor_ref, gated_ref, slope_ref, turn):
    rows, depth, width = signal_ref.shape
    piece = gated_ref.shape[0] // ctx
    count = ctx * piece
    for a in range(rows):
        first = dot(factor_ref[...], signal_ref[a], 1, 0)
        own = jnp.concatenate(
            [signal_ref[a, d * slab + offset : d * slab + offset + piece, :] for d in range(ctx)],
            axis=0,
        )
        gate = sigmoid(own.astype(F32))
        gated = first * gate
        slope_ref[a] = (gated * (1.0 - gate)).astype(BF16)
        for lane in range(width // 128):
            turn[lane, pl.ds(a, count, stride=rows), :] = gated[:, lane * 128 : (lane + 1) * 128]
    for lane in range(width // 128):
        gated_ref[:, :, lane * 128 : (lane + 1) * 128] = (
            turn[lane].reshape(count, rows, 128).astype(BF16)
        )


def first_mix(signal, factor_turned, slab, offset, ctx, after=()):
    rows, depth, width = signal.shape
    count = factor_turned.shape[0]
    block = min(16, rows)
    return call(
        functools.partial(first_mix_body, slab, offset, ctx),
        (
            jax.ShapeDtypeStruct((count, rows, width), BF16),
            jax.ShapeDtypeStruct((rows, count, width), BF16),
        ),
        (2 * rows * depth * count * width, 2 * rows * width * (depth + 2 * count)),
        (signal, factor_turned),
        [
            pl.BlockSpec((block, depth, width), lambda s: (s, 0, 0)),
            pl.BlockSpec((count, depth), lambda s: (0, 0)),
        ],
        after,
        grid=(rows // block,),
        out_specs=(
            pl.BlockSpec((count, block, width), lambda s: (0, s, 0)),
            pl.BlockSpec((block, count, width), lambda s: (s, 0, 0)),
        ),
        scratch_shapes=[pltpu.VMEM((width // 128, count * block, 128), F32)],
        name="first_mix",
    )


def tokens_of(gated_ref, t):
    ctx, _, rows, width = gated_ref.shape
    return gated_ref[:, t].reshape(ctx * rows, width)


def square_body(gated_ref, factor_ref, square_ref):
    steps, inner, _ = square_ref.shape
    for t in range(steps * inner):
        mixed = dot(factor_ref[...], tokens_of(gated_ref, t), 1, 0)
        square_ref[t // inner, t % inner : t % inner + 1, :] = to_row(
            jnp.sum(mixed * mixed, axis=1, keepdims=True)
        )


def squares(gated, factor_turned, inner, after=()):
    ctx, piece, rows, width = gated.shape
    tall = factor_turned.shape[0]
    block = min(8, piece)
    return call(
        square_body,
        jax.ShapeDtypeStruct((piece // inner, inner, tall), F32),
        (2 * piece * tall * tall * width, 2 * gated.size),
        (gated, factor_turned),
        [
            pl.BlockSpec((ctx, block, rows, width), lambda s: (0, s, 0, 0)),
            whole(factor_turned),
        ],
        after,
        grid=(piece // block,),
        out_specs=pl.BlockSpec((block // inner, inner, tall), lambda s: (s, 0, 0)),
        name="squares",
    )


def gathered(parts_ref, step, t):
    return sum(parts_ref[g, step, t : t + 1, :] for g in range(parts_ref.shape[0]))


def inverse_of(square_ref, step, t, channels):
    return lax.rsqrt(gathered(square_ref, step, t) * (1.0 / channels) + EPSILON)


def mlp_body(
    channels, carried, gated_ref, factor_ref, square_ref, gain_ref, up_ref, up_turned_ref,
    down_ref, down_turned_ref, cotangent_ref, up_in_ref, down_in_ref, gain_in_ref, *refs,
):
    (layer_ref, pull_ref, cross_ref, up_out_ref, down_out_ref, gain_out_ref,
     mixed_all, normed_all, act_all, pre_all, spread_all) = refs[carried:]
    inner = square_ref.shape[2]
    tall = factor_ref.shape[0]
    width = gain_ref.shape[1]
    hidden = up_ref.shape[1]

    @pl.when(pl.program_id(0) == 0)
    def _():
        up_out_ref[...] = up_in_ref[...]
        down_out_ref[...] = down_in_ref[...]
        gain_out_ref[...] = gain_in_ref[...]

    for t in range(inner):
        inverse = inverse_of(square_ref, 0, t, channels)
        part = slice(t * tall, (t + 1) * tall)
        mixed = dot(factor_ref[...], tokens_of(gated_ref, t), 1, 0)
        spread = to_column(inverse, width)
        mixed_all[part, :] = mixed
        spread_all[part, :] = spread
        normed_all[part, :] = (mixed * spread * gain_ref[...]).astype(BF16)
    upstream = cotangent_ref[...].reshape(inner * tall, width)
    normed = normed_all[...]
    step = min(256, hidden)
    for h in range(0, hidden, step):
        part = slice(h, h + step)
        pre = dot(normed, up_ref[:, part], 1, 0)
        back = dot(upstream, down_turned_ref[:, part], 1, 0)
        square = pre * pre
        lean = jnp.tanh(pre * (square * (TANH_SCALE * TANH_CUBIC) + TANH_SCALE))
        half = 0.5 * lean + 0.5
        act = pre * half
        act_all[:, part] = act.astype(BF16)
        bend = square * (6.0 * TANH_SCALE * TANH_CUBIC) + 2.0 * TANH_SCALE
        pre_all[:, part] = (back * (half + act * (1.0 - half) * bend)).astype(BF16)
    mixed = mixed_all[...]
    layer = mixed + dot(act_all[...], down_ref[...], 1, 0)
    layer_ref[...] = layer.astype(BF16).reshape(layer_ref.shape)
    down_out_ref[...] += dot(upstream, act_all[...], 0, 0)
    up_out_ref[...] += dot(normed, pre_all[...], 0, 0)
    grad_normed = dot(pre_all[...], up_turned_ref[...], 1, 0)
    spread = spread_all[...]
    gain = gain_ref[...]
    weighed = grad_normed * mixed
    gain_out_ref[...] += jnp.sum(weighed * spread, axis=0, keepdims=True)
    cross = jnp.sum(weighed * gain, axis=1, keepdims=True)
    for t in range(inner):
        cross_ref[0, t : t + 1, :] = to_row(cross[t * tall : (t + 1) * tall])
    pull_ref[...] = (grad_normed * gain * spread).astype(BF16).reshape(pull_ref.shape)


def mlp(gated, part, factor_turned, square, gain, up, up_turned, down, down_turned, cotangent,
        first_piece, sums, layer_pull, channels, after=()):
    ctx, _, rows, width = gated.shape
    groups, _, inner, tall = square.shape
    hidden = up.shape[1]
    begin, piece = part
    steps, skip = piece // inner, begin // inner
    start = (first_piece + begin) // inner
    tokens = inner * tall
    by_token = pl.BlockSpec((inner, tall, width), lambda s: (s + start, 0, 0))
    stays = pl.BlockSpec(memory_space=pl.ANY)
    full = jax.ShapeDtypeStruct(cotangent.shape, BF16)
    carried = len(layer_pull)
    aliases = {9: 3, 10: 4, 11: 5}
    for i in range(carried):
        aliases[12 + i] = i
    return call(
        functools.partial(mlp_body, channels, carried),
        (
            full,
            full,
            jax.ShapeDtypeStruct((steps, inner, tall), F32),
            *(jax.ShapeDtypeStruct(array.shape, F32) for array in sums),
        ),
        (12 * piece * tall * width * hidden, 8 * piece * tall * width),
        (gated, factor_turned, square, gain, up, up_turned, down, down_turned, cotangent, *sums,
         *layer_pull),
        [
            pl.BlockSpec((ctx, inner, rows, width), lambda s: (0, s + skip, 0, 0)),
            whole(factor_turned),
            pl.BlockSpec((groups, 1, inner, tall), lambda s: (0, s + skip, 0, 0)),
            whole(gain), whole(up), whole(up_turned), whole(down), whole(down_turned),
            by_token,
            *(whole(array) for array in sums),
            *([stays] * carried),
        ],
        after,
        grid=(steps,),
        out_specs=(
            by_token, by_token,
            pl.BlockSpec((1, inner, tall), lambda s: (s, 0, 0)),
            *(whole(array) for array in sums),
        ),
        scratch_shapes=[
            pltpu.VMEM((tokens, width), F32),
            pltpu.VMEM((tokens, width), BF16),
            pltpu.VMEM((tokens, hidden), BF16),
            pltpu.VMEM((tokens, hidden), BF16),
            pltpu.VMEM((tokens, width), F32),
        ],
        input_output_aliases=aliases,
        name="mlp",
    )


def second_body(
    channels, gated_ref, factor_ref, factor_turned_ref, square_ref, cross_ref, pull_ref,
    cotangent_ref, sum_in_ref, moved_ref, sum_out_ref,
):
    _, steps, inner, tall = square_ref.shape
    ctx, _, rows, width = gated_ref.shape

    @pl.when(pl.program_id(0) == 0)
    def _():
        sum_out_ref[...] = sum_in_ref[...]

    total = sum_out_ref[...]
    for t in range(steps * inner):
        gated = tokens_of(gated_ref, t)
        mixed = dot(factor_turned_ref[...], gated, 1, 0)
        inverse = inverse_of(square_ref, t // inner, t % inner, channels)
        cross = gathered(cross_ref, t // inner, t % inner)
        weight = to_column(inverse * inverse * inverse * cross * (1.0 / channels), width)
        grad = (
            cotangent_ref[t].astype(F32) + pull_ref[t].astype(F32) - mixed * weight
        ).astype(BF16)
        total += dot(gated, grad, 1, 1)
        moved_ref[:, t] = dot(factor_ref[...], grad, 1, 0).astype(BF16).reshape(ctx, rows, width)
    sum_out_ref[...] = total


def second(gated, factor, factor_turned, square, cross, pull, cotangent, first_piece, total,
           channels, after=()):
    ctx, piece, rows, width = gated.shape
    groups, steps, inner, tall = square.shape
    block = max(size for size in (4, 2, 1) if steps % size == 0)
    count = block * inner
    start = first_piece // count
    by_piece = pl.BlockSpec((groups, block, inner, tall), lambda s: (0, s, 0, 0))
    by_token = pl.BlockSpec((count, tall, width), lambda s: (s + start, 0, 0))
    return call(
        functools.partial(second_body, channels),
        (
            jax.ShapeDtypeStruct(gated.shape, BF16),
            jax.ShapeDtypeStruct(total.shape, F32),
        ),
        (6 * piece * tall * tall * width, 8 * gated.size),
        (gated, factor, factor_turned, square, cross, pull, cotangent, total),
        [
            pl.BlockSpec((ctx, count, rows, width), lambda s: (0, s, 0, 0)),
            whole(factor), whole(factor_turned), by_piece, by_piece, by_token, by_token,
            whole(total),
        ],
        after,
        grid=(steps // block,),
        out_specs=(
            pl.BlockSpec((ctx, count, rows, width), lambda s: (0, s, 0, 0)),
            whole(total),
        ),
        input_output_aliases={7: 1},
        name="second",
    )


def gate_body(slab, offset, ctx, carried, moved_ref, signal_ref, slope_ref, *refs):
    first_ref, gate_ref, sum_ref, turn, total_ref = refs[carried:]
    rows, depth, width = signal_ref.shape
    count = moved_ref.shape[0]
    piece = count // ctx

    @pl.when(pl.program_id(0) == 0)
    def _():
        total_ref[...] = jnp.zeros_like(total_ref)

    for lane in range(width // 128):
        turn[lane] = (
            moved_ref[:, :, lane * 128 : (lane + 1) * 128]
            .astype(F32)
            .reshape(count * rows, 128)
        )
    total = total_ref[...]
    for a in range(rows):
        grad = jnp.concatenate(
            [turn[lane, pl.ds(a, count, stride=rows), :] for lane in range(width // 128)], axis=1
        )
        own = jnp.concatenate(
            [signal_ref[a, d * slab + offset : d * slab + offset + piece, :] for d in range(ctx)],
            axis=0,
        )
        first = (grad * sigmoid(own.astype(F32))).astype(BF16)
        first_ref[a] = first
        gate_ref[a] = (grad * slope_ref[a].astype(F32)).astype(BF16)
        total += dot(signal_ref[a], first, 1, 1)
    total_ref[...] = total

    @pl.when(pl.program_id(0) == pl.num_programs(0) - 1)
    def _():
        sum_ref[...] = total_ref[...].astype(BF16).reshape(sum_ref.shape)


def gate(moved, signal, slope, slab, k, pieces, sums, ctx, after=()):
    rows, depth, width = signal.shape
    count = moved.shape[0]
    block = min(16, rows)
    by_row = pl.BlockSpec((block, count, width), lambda s: (s, 0, 0))
    return call(
        functools.partial(gate_body, slab, k * (count // ctx), ctx, len(sums)),
        (
            jax.ShapeDtypeStruct((rows, count, width), BF16),
            jax.ShapeDtypeStruct((rows, count, width), BF16),
            jax.ShapeDtypeStruct((ctx, pieces, depth // ctx, count), BF16),
        ),
        (2 * rows * depth * count * width, 2 * rows * width * (depth + 4 * count)),
        (moved, signal, slope, *sums),
        [
            pl.BlockSpec((count, block, width), lambda s: (0, s, 0)),
            pl.BlockSpec((block, depth, width), lambda s: (s, 0, 0)),
            by_row,
            *([pl.BlockSpec(memory_space=pl.ANY)] * len(sums)),
        ],
        after,
        grid=(rows // block,),
        out_specs=(
            by_row,
            by_row,
            pl.BlockSpec((ctx, 1, depth // ctx, count), lambda s: (0, k, 0, 0)),
        ),
        scratch_shapes=[
            pltpu.VMEM((width // 128, count * block, 128), F32),
            pltpu.VMEM((depth, count), F32),
        ],
        input_output_aliases={3: 2} if sums else {},
        name="gate",
    )


def signal_body(offsets, slab, ctx, factor_ref, *refs):
    pieces = len(offsets)
    firsts, gates, out_ref = refs[:pieces], refs[pieces : 2 * pieces], refs[-1]
    for a in range(out_ref.shape[0]):
        grads = jnp.concatenate([first[a] for first in firsts], axis=0)
        total = dot(factor_ref[...], grads, 1, 0)
        for gate_ref, offset in zip(gates, offsets):
            piece = gate_ref.shape[1] // ctx
            for d in range(ctx):
                place = slice(d * slab + offset, d * slab + offset + piece)
                out_ref[a, place, :] = (
                    total[place] + gate_ref[a, d * piece : (d + 1) * piece, :].astype(F32)
                ).astype(BF16)


def signal_grad(factor, firsts, gates, offsets, slab, ctx, after=()):
    rows, _, width = firsts[0].shape
    depth = factor.shape[0]
    block = min(4, rows)
    by_row = [pl.BlockSpec((block, *array.shape[1:]), lambda s: (s, 0, 0)) for array in firsts]
    return call(
        functools.partial(signal_body, offsets, slab, ctx),
        jax.ShapeDtypeStruct((rows, depth, width), BF16),
        (2 * rows * depth * depth * width, 6 * rows * depth * width),
        (factor, *firsts, *gates),
        [whole(factor), *by_row, *by_row],
        after,
        grid=(rows // block,),
        out_specs=pl.BlockSpec((block, depth, width), lambda s: (s, 0, 0)),
        name="signal_grad",
    )


def fold_body(mine_ref, values_ref, got_ref, *refs):
    del mine_ref
    refs[-1][...] = values_ref[...].reshape(refs[-1].shape) + got_ref[...].astype(F32)


def fold(values, got, mine, after=()):
    blocks, _, rows, columns = values.shape
    return pl.pallas_call(
        fold_body,
        out_shape=jax.ShapeDtypeStruct((blocks, rows, columns), F32),
        grid_spec=pltpu.PrefetchScalarGridSpec(
            num_scalar_prefetch=1,
            grid=(blocks,),
            in_specs=[
                pl.BlockSpec((1, 1, rows, columns), lambda s, mine: (s, mine[0], 0, 0)),
                pl.BlockSpec((1, rows, columns), lambda s, mine: (s, 0, 0)),
                *([pl.BlockSpec(memory_space=pl.ANY)] * len(after)),
            ],
            out_specs=pl.BlockSpec((1, rows, columns), lambda s, mine: (s, 0, 0)),
        ),
        cost_estimate=pl.CostEstimate(
            flops=got.size, bytes_accessed=10 * got.size, transcendentals=0
        ),
        name="fold",
    )(mine.reshape(1), values, got, *after)


def scatter_total(values, ctx, afters):
    if ctx & (ctx - 1):
        return lax.psum_scatter(values, "ctx", scatter_dimension=0, tiled=False)
    me = lax.axis_index("ctx")
    bit, step = 1, 0
    while bit < ctx:
        halves = values.reshape((-1, 2) + values.shape[1:])
        mine = (me // bit) % 2
        give = lax.dynamic_index_in_dim(halves, 1 - mine, 1, keepdims=False)
        got = lax.ppermute(give.astype(BF16), "ctx", [(i, i ^ bit) for i in range(ctx)])
        values = fold(halves, got, mine, afters[step] if step < len(afters) else ())
        bit, step = bit * 2, step + 1
    return values[0]


def block_total_body(scale, parts_ref, total_ref):
    ctx, pieces, _, count = parts_ref.shape
    size = count // ctx
    for k in range(pieces):
        total = parts_ref[0, k].astype(F32)
        for source in range(1, ctx):
            total += parts_ref[source, k].astype(F32)
        total *= scale
        for d in range(ctx):
            place = (d * pieces + k) * size
            total_ref[:, place : place + size] = total[:, d * size : (d + 1) * size]


def block_total(parts, scale, after=()):
    _, pieces, rows, count = parts.shape
    return call(
        functools.partial(block_total_body, scale),
        jax.ShapeDtypeStruct((rows, pieces * count), F32),
        (parts.size, 4 * parts.size),
        (parts,),
        [whole(parts)],
        after,
        grid=(1,),
        out_specs=pl.BlockSpec((rows, pieces * count), lambda s: (0, 0)),
        name="block_total",
    )


def from_groups(partial_value):
    return lax.all_gather(partial_value, "ch")


def exchange(block):
    return lax.all_to_all(block, "ctx", split_axis=0, concat_axis=0, tiled=True)


def shards(ctx, channels, token_count, signal, factor_first, factor_second, up_weight,
           down_weight, norm_gain, cotangent):
    rows, depth, width = signal.shape
    slab, tall, _ = cotangent.shape
    first, factor = factor_first[0], factor_second[0]
    up, down = up_weight[0], down_weight[0]
    hidden = up.shape[1]
    factor_turned, up_turned, down_turned = factor.T, up.T, down.T
    pieces = 2 if slab % 32 == 0 else 1
    size = slab // pieces
    unit = min(16, size)
    inner = 2
    by_owner = first.reshape(depth, ctx, pieces, size)
    columns = [by_owner[:, :, k].reshape(depth, ctx * size) for k in range(pieces)]
    sums = (
        jnp.zeros((width, hidden), F32),
        jnp.zeros((width, hidden), F32),
        jnp.zeros((1, width), F32),
    )
    layer_pull = ()
    second_sum = jnp.zeros((tall, tall), F32)
    slopes, arrived, moved = [], [], []
    for k in range(pieces):
        gated, slope = first_mix(signal, columns[k].T, slab, k * size, ctx)
        slopes.append(slope)
        arrived.append(exchange(gated).reshape(ctx, size, rows, width))
    waits = ()
    for k in range(pieces):
        square = from_groups(squares(arrived[k], factor_turned, inner, waits))
        crosses = []
        for begin in range(0, size, unit):
            layer, pull, cross, *sums = mlp(
                arrived[k], (begin, unit), factor_turned, square, norm_gain, up, up_turned, down,
                down_turned, cotangent, k * size, sums, layer_pull, channels,
            )
            layer_pull = (layer, pull)
            crosses.append(cross)
        cross = from_groups(jnp.concatenate(crosses))
        back, second_sum = second(
            arrived[k], factor, factor_turned, square, cross, pull, cotangent, k * size,
            second_sum, channels,
        )
        waits = (back,)
        moved.append(exchange(back.reshape(ctx * size, rows, width)))
    up_sum, down_sum, gain_sum = sums
    gain_width = width // ctx
    packed = jnp.concatenate(
        [
            up_sum.reshape(ctx, gain_width * (hidden // tall), tall),
            down_sum.T.reshape(ctx, hidden * width // (ctx * tall), tall),
            second_sum.reshape(ctx, tall // ctx, tall),
            jnp.pad(gain_sum.reshape(ctx, 1, gain_width), ((0, 0), (0, 15), (0, tall - gain_width))),
        ],
        axis=1,
    )
    sums, firsts, gates = (), [], []
    for k in range(pieces):
        first_grad, gate_grad, first_sum = gate(
            moved[k], signal, slopes[k], slab, k, pieces, sums, ctx
        )
        sums = (first_sum,)
        firsts.append(first_grad)
        gates.append(gate_grad)
    packed = scatter_total(packed, ctx, ((firsts[0],), (firsts[-1],)))
    parts = exchange(first_sum)
    grad_signal = signal_grad(
        jnp.concatenate(columns, axis=1), firsts, gates, tuple(k * size for k in range(pieces)),
        slab, ctx,
    )
    scale = token_count ** (-0.5)
    grad_first = block_total(parts, scale, (grad_signal,))
    packed = packed * scale
    a = gain_width * (hidden // tall)
    b = a + hidden * width // (ctx * tall)
    c = b + tall // ctx
    return (
        layer,
        grad_signal,
        grad_first[None],
        packed[b:c][None],
        packed[:a].reshape(1, gain_width, hidden),
        packed[a:b].reshape(1, hidden // ctx, width),
        packed[c, :gain_width][None],
    )


def solution(mesh):
    placed = (
        P("ctx", None, "ch"),
        P("ch", None, None),
        P("ch", None, None),
        P("ch", None, None),
        P("ch", None, None),
        P("ch", None),
        P("ctx", None, "ch"),
    )

    def layer(signal, factor_first, factor_second, up_weight, down_weight, norm_gain, cotangent):
        body = functools.partial(
            shards, mesh.shape["ctx"], signal.shape[2], signal.shape[0] * signal.shape[1]
        )
        return jax.shard_map(
            body,
            mesh=mesh,
            in_specs=placed,
            out_specs=(
                P("ctx", None, "ch"),
                P("ctx", None, "ch"),
                P("ch", "ctx", None),
                P("ch", "ctx", None),
                P("ch", "ctx", None),
                P("ch", "ctx", None),
                P("ch", "ctx"),
            ),
            check_vma=False,
        )(signal, factor_first, factor_second, up_weight, down_weight, norm_gain, cotangent)

    return layer
```

```python
import functools

import jax
import jax.numpy as jnp
from jax import lax
from jax.experimental import pallas as pl
from jax.experimental.pallas import tpu as pltpu
from jax.sharding import PartitionSpec as P

EPSILON = 1e-05
TANH_SCALE = 0.7978845608028654
TANH_CUBIC = 0.044715
BF16 = jnp.bfloat16
F32 = jnp.float32
MIB = 1024 * 1024


def sigmoid(values):
    return 0.5 * jnp.tanh(0.5 * values) + 0.5


def dot(left, right, left_dim, right_dim):
    return lax.dot_general(
        left, right, (((left_dim,), (right_dim,)), ((), ())), preferred_element_type=F32
    )


def to_row(column):
    return jnp.broadcast_to(column, (column.shape[0], 128)).T[0:1, :]


def to_column(row, width):
    spread = jnp.broadcast_to(row, (128, row.shape[1])).T
    return jnp.concatenate([spread] * (width // 128), axis=1)


def call(body, out_shape, cost, operands, in_specs, after=(), vmem=56, **options):
    flops, bytes_accessed = cost
    given, waits = len(operands), len(after)

    def ordered(*refs):
        body(*refs[:given], *refs[given + waits :])

    return pl.pallas_call(
        ordered,
        out_shape=out_shape,
        in_specs=[*in_specs, *([pl.BlockSpec(memory_space=pl.ANY)] * waits)],
        compiler_params=pltpu.CompilerParams(vmem_limit_bytes=vmem * MIB),
        cost_estimate=pl.CostEstimate(
            flops=int(flops), bytes_accessed=int(bytes_accessed), transcendentals=0
        ),
        **options,
    )(*operands, *after)


def whole(array):
    return pl.BlockSpec(array.shape, lambda s: (0,) * array.ndim)


def first_mix_body(slab, offset, ctx, signal_ref, factor_ref, gated_ref, slope_ref, turn):
    rows, depth, width = signal_ref.shape
    piece = gated_ref.shape[0] // ctx
    count = ctx * piece
    for a in range(rows):
        first = dot(factor_ref[...], signal_ref[a], 1, 0)
        own = jnp.concatenate(
            [signal_ref[a, d * slab + offset : d * slab + offset + piece, :] for d in range(ctx)],
            axis=0,
        )
        gate = sigmoid(own.astype(F32))
        gated = first * gate
        slope_ref[a] = (gated * (1.0 - gate)).astype(BF16)
        for lane in range(width // 128):
            turn[lane, pl.ds(a, count, stride=rows), :] = gated[:, lane * 128 : (lane + 1) * 128]
    for lane in range(width // 128):
        gated_ref[:, :, lane * 128 : (lane + 1) * 128] = (
            turn[lane].reshape(count, rows, 128).astype(BF16)
        )


def first_mix(signal, factor_turned, slab, offset, ctx, after=()):
    rows, depth, width = signal.shape
    count = factor_turned.shape[0]
    block = min(16, rows)
    return call(
        functools.partial(first_mix_body, slab, offset, ctx),
        (
            jax.ShapeDtypeStruct((count, rows, width), BF16),
            jax.ShapeDtypeStruct((rows, count, width), BF16),
        ),
        (2 * rows * depth * count * width, 2 * rows * width * (depth + 2 * count)),
        (signal, factor_turned),
        [
            pl.BlockSpec((block, depth, width), lambda s: (s, 0, 0)),
            pl.BlockSpec((count, depth), lambda s: (0, 0)),
        ],
        after,
        grid=(rows // block,),
        out_specs=(
            pl.BlockSpec((count, block, width), lambda s: (0, s, 0)),
            pl.BlockSpec((block, count, width), lambda s: (s, 0, 0)),
        ),
        scratch_shapes=[pltpu.VMEM((width // 128, count * block, 128), F32)],
        name="first_mix",
    )


def tokens_of(gated_ref, t):
    ctx, _, rows, width = gated_ref.shape
    return gated_ref[:, t].reshape(ctx * rows, width)


def square_body(gated_ref, factor_ref, square_ref):
    steps, inner, _ = square_ref.shape
    for t in range(steps * inner):
        mixed = dot(factor_ref[...], tokens_of(gated_ref, t), 1, 0)
        square_ref[t // inner, t % inner : t % inner + 1, :] = to_row(
            jnp.sum(mixed * mixed, axis=1, keepdims=True)
        )


def squares(gated, factor_turned, inner, after=()):
    ctx, piece, rows, width = gated.shape
    tall = factor_turned.shape[0]
    block = min(8, piece)
    return call(
        square_body,
        jax.ShapeDtypeStruct((piece // inner, inner, tall), F32),
        (2 * piece * tall * tall * width, 2 * gated.size),
        (gated, factor_turned),
        [
            pl.BlockSpec((ctx, block, rows, width), lambda s: (0, s, 0, 0)),
            whole(factor_turned),
        ],
        after,
        grid=(piece // block,),
        out_specs=pl.BlockSpec((block // inner, inner, tall), lambda s: (s, 0, 0)),
        name="squares",
    )


def gathered(parts_ref, step, t):
    return sum(parts_ref[g, step, t : t + 1, :] for g in range(parts_ref.shape[0]))


def inverse_of(square_ref, step, t, channels):
    return lax.rsqrt(gathered(square_ref, step, t) * (1.0 / channels) + EPSILON)


def mlp_body(
    channels, carried, gated_ref, factor_ref, square_ref, gain_ref, up_ref, up_turned_ref,
    down_ref, down_turned_ref, cotangent_ref, up_in_ref, down_in_ref, gain_in_ref, *refs,
):
    (layer_ref, pull_ref, cross_ref, up_out_ref, down_out_ref, gain_out_ref,
     mixed_all, normed_all, act_all, pre_all, spread_all) = refs[carried:]
    inner = square_ref.shape[2]
    tall = factor_ref.shape[0]
    width = gain_ref.shape[1]
    hidden = up_ref.shape[1]

    @pl.when(pl.program_id(0) == 0)
    def _():
        up_out_ref[...] = up_in_ref[...]
        down_out_ref[...] = down_in_ref[...]
        gain_out_ref[...] = gain_in_ref[...]

    for t in range(inner):
        inverse = inverse_of(square_ref, 0, t, channels)
        part = slice(t * tall, (t + 1) * tall)
        mixed = dot(factor_ref[...], tokens_of(gated_ref, t), 1, 0)
        spread = to_column(inverse, width)
        mixed_all[part, :] = mixed
        spread_all[part, :] = spread
        normed_all[part, :] = (mixed * spread * gain_ref[...]).astype(BF16)
    upstream = cotangent_ref[...].reshape(inner * tall, width)
    normed = normed_all[...]
    step = min(256, hidden)
    for h in range(0, hidden, step):
        part = slice(h, h + step)
        pre = dot(normed, up_ref[:, part], 1, 0)
        back = dot(upstream, down_turned_ref[:, part], 1, 0)
        square = pre * pre
        lean = jnp.tanh(pre * (square * (TANH_SCALE * TANH_CUBIC) + TANH_SCALE))
        half = 0.5 * lean + 0.5
        act = pre * half
        act_all[:, part] = act.astype(BF16)
        bend = square * (6.0 * TANH_SCALE * TANH_CUBIC) + 2.0 * TANH_SCALE
        pre_all[:, part] = (back * (half + act * (1.0 - half) * bend)).astype(BF16)
    mixed = mixed_all[...]
    layer = mixed + dot(act_all[...], down_ref[...], 1, 0)
    layer_ref[...] = layer.astype(BF16).reshape(layer_ref.shape)
    down_out_ref[...] += dot(upstream, act_all[...], 0, 0)
    up_out_ref[...] += dot(normed, pre_all[...], 0, 0)
    grad_normed = dot(pre_all[...], up_turned_ref[...], 1, 0)
    spread = spread_all[...]
    gain = gain_ref[...]
    weighed = grad_normed * mixed
    gain_out_ref[...] += jnp.sum(weighed * spread, axis=0, keepdims=True)
    cross = jnp.sum(weighed * gain, axis=1, keepdims=True)
    for t in range(inner):
        cross_ref[0, t : t + 1, :] = to_row(cross[t * tall : (t + 1) * tall])
    pull_ref[...] = (grad_normed * gain * spread).astype(BF16).reshape(pull_ref.shape)


def mlp(gated, part, factor_turned, square, gain, up, up_turned, down, down_turned, cotangent,
        first_piece, sums, layer_pull, channels, after=()):
    ctx, _, rows, width = gated.shape
    groups, _, inner, tall = square.shape
    hidden = up.shape[1]
    begin, piece = part
    steps, skip = piece // inner, begin // inner
    start = (first_piece + begin) // inner
    tokens = inner * tall
    by_token = pl.BlockSpec((inner, tall, width), lambda s: (s + start, 0, 0))
    stays = pl.BlockSpec(memory_space=pl.ANY)
    full = jax.ShapeDtypeStruct(cotangent.shape, BF16)
    carried = len(layer_pull)
    aliases = {9: 3, 10: 4, 11: 5}
    for i in range(carried):
        aliases[12 + i] = i
    return call(
        functools.partial(mlp_body, channels, carried),
        (
            full,
            full,
            jax.ShapeDtypeStruct((steps, inner, tall), F32),
            *(jax.ShapeDtypeStruct(array.shape, F32) for array in sums),
        ),
        (12 * piece * tall * width * hidden, 8 * piece * tall * width),
        (gated, factor_turned, square, gain, up, up_turned, down, down_turned, cotangent, *sums,
         *layer_pull),
        [
            pl.BlockSpec((ctx, inner, rows, width), lambda s: (0, s + skip, 0, 0)),
            whole(factor_turned),
            pl.BlockSpec((groups, 1, inner, tall), lambda s: (0, s + skip, 0, 0)),
            whole(gain), whole(up), whole(up_turned), whole(down), whole(down_turned),
            by_token,
            *(whole(array) for array in sums),
            *([stays] * carried),
        ],
        after,
        grid=(steps,),
        out_specs=(
            by_token, by_token,
            pl.BlockSpec((1, inner, tall), lambda s: (s, 0, 0)),
            *(whole(array) for array in sums),
        ),
        scratch_shapes=[
            pltpu.VMEM((tokens, width), F32),
            pltpu.VMEM((tokens, width), BF16),
            pltpu.VMEM((tokens, hidden), BF16),
            pltpu.VMEM((tokens, hidden), BF16),
            pltpu.VMEM((tokens, width), F32),
        ],
        input_output_aliases=aliases,
        name="mlp",
    )


def second_body(
    channels, gated_ref, factor_ref, factor_turned_ref, square_ref, cross_ref, pull_ref,
    cotangent_ref, sum_in_ref, moved_ref, sum_out_ref,
):
    _, steps, inner, tall = square_ref.shape
    ctx, _, rows, width = gated_ref.shape

    @pl.when(pl.program_id(0) == 0)
    def _():
        sum_out_ref[...] = sum_in_ref[...]

    total = sum_out_ref[...]
    for t in range(steps * inner):
        gated = tokens_of(gated_ref, t)
        mixed = dot(factor_turned_ref[...], gated, 1, 0)
        inverse = inverse_of(square_ref, t // inner, t % inner, channels)
        cross = gathered(cross_ref, t // inner, t % inner)
        weight = to_column(inverse * inverse * inverse * cross * (1.0 / channels), width)
        grad = (
            cotangent_ref[t].astype(F32) + pull_ref[t].astype(F32) - mixed * weight
        ).astype(BF16)
        total += dot(gated, grad, 1, 1)
        moved_ref[:, t] = dot(factor_ref[...], grad, 1, 0).astype(BF16).reshape(ctx, rows, width)
    sum_out_ref[...] = total


def second(gated, factor, factor_turned, square, cross, pull, cotangent, first_piece, total,
           channels, after=()):
    ctx, piece, rows, width = gated.shape
    groups, steps, inner, tall = square.shape
    block = max(size for size in (4, 2, 1) if steps % size == 0)
    count = block * inner
    start = first_piece // count
    by_piece = pl.BlockSpec((groups, block, inner, tall), lambda s: (0, s, 0, 0))
    by_token = pl.BlockSpec((count, tall, width), lambda s: (s + start, 0, 0))
    return call(
        functools.partial(second_body, channels),
        (
            jax.ShapeDtypeStruct(gated.shape, BF16),
            jax.ShapeDtypeStruct(total.shape, F32),
        ),
        (6 * piece * tall * tall * width, 8 * gated.size),
        (gated, factor, factor_turned, square, cross, pull, cotangent, total),
        [
            pl.BlockSpec((ctx, count, rows, width), lambda s: (0, s, 0, 0)),
            whole(factor), whole(factor_turned), by_piece, by_piece, by_token, by_token,
            whole(total),
        ],
        after,
        grid=(steps // block,),
        out_specs=(
            pl.BlockSpec((ctx, count, rows, width), lambda s: (0, s, 0, 0)),
            whole(total),
        ),
        input_output_aliases={7: 1},
        name="second",
    )


def gate_body(slab, offset, ctx, carried, moved_ref, signal_ref, slope_ref, *refs):
    first_ref, gate_ref, sum_ref, turn, total_ref = refs[carried:]
    rows, depth, width = signal_ref.shape
    count = moved_ref.shape[0]
    piece = count // ctx

    @pl.when(pl.program_id(0) == 0)
    def _():
        total_ref[...] = jnp.zeros_like(total_ref)

    for lane in range(width // 128):
        turn[lane] = (
            moved_ref[:, :, lane * 128 : (lane + 1) * 128]
            .astype(F32)
            .reshape(count * rows, 128)
        )
    total = total_ref[...]
    for a in range(rows):
        grad = jnp.concatenate(
            [turn[lane, pl.ds(a, count, stride=rows), :] for lane in range(width // 128)], axis=1
        )
        own = jnp.concatenate(
            [signal_ref[a, d * slab + offset : d * slab + offset + piece, :] for d in range(ctx)],
            axis=0,
        )
        first = (grad * sigmoid(own.astype(F32))).astype(BF16)
        first_ref[a] = first
        gate_ref[a] = (grad * slope_ref[a].astype(F32)).astype(BF16)
        total += dot(signal_ref[a], first, 1, 1)
    total_ref[...] = total

    @pl.when(pl.program_id(0) == pl.num_programs(0) - 1)
    def _():
        sum_ref[...] = total_ref[...].astype(BF16).reshape(sum_ref.shape)


def gate(moved, signal, slope, slab, k, pieces, sums, ctx, after=()):
    rows, depth, width = signal.shape
    count = moved.shape[0]
    block = min(16, rows)
    by_row = pl.BlockSpec((block, count, width), lambda s: (s, 0, 0))
    return call(
        functools.partial(gate_body, slab, k * (count // ctx), ctx, len(sums)),
        (
            jax.ShapeDtypeStruct((rows, count, width), BF16),
            jax.ShapeDtypeStruct((rows, count, width), BF16),
            jax.ShapeDtypeStruct(sums[0].shape, BF16)
            if sums
            else jax.ShapeDtypeStruct((ctx, pieces * (depth // ctx), count), BF16),
        ),
        (2 * rows * depth * count * width, 2 * rows * width * (depth + 4 * count)),
        (moved, signal, slope, *sums),
        [
            pl.BlockSpec((count, block, width), lambda s: (0, s, 0)),
            pl.BlockSpec((block, depth, width), lambda s: (s, 0, 0)),
            by_row,
            *([pl.BlockSpec(memory_space=pl.ANY)] * len(sums)),
        ],
        after,
        grid=(rows // block,),
        out_specs=(
            by_row,
            by_row,
            pl.BlockSpec((ctx, depth // ctx, count), lambda s: (0, k, 0)),
        ),
        scratch_shapes=[
            pltpu.VMEM((width // 128, count * block, 128), F32),
            pltpu.VMEM((depth, count), F32),
        ],
        input_output_aliases={3: 2} if sums else {},
        name="gate",
    )


def signal_body(offsets, slab, ctx, factor_ref, *refs):
    pieces = len(offsets)
    firsts, gates, out_ref = refs[:pieces], refs[pieces : 2 * pieces], refs[-1]
    for a in range(out_ref.shape[0]):
        grads = jnp.concatenate([first[a] for first in firsts], axis=0)
        total = dot(factor_ref[...], grads, 1, 0)
        for gate_ref, offset in zip(gates, offsets):
            piece = gate_ref.shape[1] // ctx
            for d in range(ctx):
                place = slice(d * slab + offset, d * slab + offset + piece)
                out_ref[a, place, :] = (
                    total[place] + gate_ref[a, d * piece : (d + 1) * piece, :].astype(F32)
                ).astype(BF16)


def signal_grad(factor, firsts, gates, offsets, slab, ctx, after=()):
    rows, _, width = firsts[0].shape
    depth = factor.shape[0]
    block = min(8, rows)
    by_row = [pl.BlockSpec((block, *array.shape[1:]), lambda s: (s, 0, 0)) for array in firsts]
    return call(
        functools.partial(signal_body, offsets, slab, ctx),
        jax.ShapeDtypeStruct((rows, depth, width), BF16),
        (2 * rows * depth * depth * width, 6 * rows * depth * width),
        (factor, *firsts, *gates),
        [whole(factor), *by_row, *by_row],
        after,
        grid=(rows // block,),
        out_specs=pl.BlockSpec((block, depth, width), lambda s: (s, 0, 0)),
        name="signal_grad",
    )


def fold_body(scale, mine_ref, values_ref, got_ref, *refs):
    del mine_ref
    total = values_ref[...].reshape(refs[-1].shape) + got_ref[...].astype(F32)
    refs[-1][...] = total * scale


def fold(values, got, mine, scale, after=()):
    blocks, _, rows, columns = values.shape
    return pl.pallas_call(
        functools.partial(fold_body, scale),
        out_shape=jax.ShapeDtypeStruct((blocks, rows, columns), F32),
        grid_spec=pltpu.PrefetchScalarGridSpec(
            num_scalar_prefetch=1,
            grid=(blocks,),
            in_specs=[
                pl.BlockSpec((1, 1, rows, columns), lambda s, mine: (s, mine[0], 0, 0)),
                pl.BlockSpec((1, rows, columns), lambda s, mine: (s, 0, 0)),
                *([pl.BlockSpec(memory_space=pl.ANY)] * len(after)),
            ],
            out_specs=pl.BlockSpec((1, rows, columns), lambda s, mine: (s, 0, 0)),
        ),
        compiler_params=pltpu.CompilerParams(vmem_limit_bytes=56 * MIB),
        cost_estimate=pl.CostEstimate(
            flops=got.size, bytes_accessed=10 * got.size, transcendentals=0
        ),
        name="fold",
    )(mine.reshape(1), values, got, *after)


class Halving:
    def __init__(self, values, ctx, scale):
        self.ctx, self.bit, self.scale = ctx, 1, scale
        self.values = values
        self.halve()

    def halve(self):
        self.halves = self.values.reshape((-1, 2) + self.values.shape[1:])
        self.mine = (lax.axis_index("ctx") // self.bit) % 2
        self.give = lax.dynamic_index_in_dim(
            self.halves, 1 - self.mine, 1, keepdims=False
        ).astype(BF16)

    def send(self):
        bit = self.bit
        self.got = lax.ppermute(self.give, "ctx", [(i, i ^ bit) for i in range(self.ctx)])
        return self.got

    def keep(self, after=()):
        self.bit = 2 * self.bit
        scale = 1.0 if self.bit < self.ctx else self.scale
        self.values = fold(self.halves, self.got, self.mine, scale, after)
        if self.bit < self.ctx:
            self.halve()

    def finish(self, after=()):
        while self.bit < self.ctx:
            self.send()
            self.keep(after)
        return self.values[0]


def block_total_body(pieces, ctx, scale, parts_ref, first_ref, *rest):
    rows = first_ref.shape[0]
    count = parts_ref.shape[2]
    size = count // ctx

    def total_of(start, stop):
        total = parts_ref[0, start:stop].astype(F32)
        for source in range(1, ctx):
            total += parts_ref[source, start:stop].astype(F32)
        return total * scale

    for k in range(pieces):
        total = total_of(k * rows, (k + 1) * rows)
        for d in range(ctx):
            place = (d * pieces + k) * size
            first_ref[:, place : place + size] = total[:, d * size : (d + 1) * size]
    if rest:
        rest[0][...] = total_of(pieces * rows, parts_ref.shape[1])


def block_total(parts, pieces, ctx, scale, after=()):
    _, all_rows, count = parts.shape
    depth = pieces * count
    more = all_rows - pieces * (depth // ctx)
    shapes = [jax.ShapeDtypeStruct((depth // ctx, depth), F32)]
    if more:
        shapes.append(jax.ShapeDtypeStruct((more, count), F32))
    return call(
        functools.partial(block_total_body, pieces, ctx, scale),
        tuple(shapes),
        (parts.size, 4 * parts.size),
        (parts,),
        [whole(parts)],
        after,
        grid=(1,),
        out_specs=tuple(pl.BlockSpec(shape.shape, lambda s: (0, 0)) for shape in shapes),
        name="block_total",
    )


def hold(array, after):
    return pl.pallas_call(
        lambda *refs: None,
        out_shape=jax.ShapeDtypeStruct(array.shape, array.dtype),
        in_specs=[pl.BlockSpec(memory_space=pl.ANY)] * (1 + len(after)),
        out_specs=pl.BlockSpec(memory_space=pl.ANY),
        input_output_aliases={0: 0},
        compiler_params=pltpu.CompilerParams(vmem_limit_bytes=56 * MIB),
        name="hold",
    )(array, *after)


def from_groups(partial_value):
    return lax.all_gather(partial_value, "ch")


def exchange(block):
    return lax.all_to_all(block, "ctx", split_axis=0, concat_axis=0, tiled=True)


def shards(ctx, channels, token_count, signal, factor_first, factor_second, up_weight,
           down_weight, norm_gain, cotangent):
    rows, depth, width = signal.shape
    slab, tall, _ = cotangent.shape
    first, factor = factor_first[0], factor_second[0]
    up, down = up_weight[0], down_weight[0]
    hidden = up.shape[1]
    factor_turned, up_turned, down_turned = factor.T, up.T, down.T
    pieces = 2 if slab % 32 == 0 else 1
    size = slab // pieces
    unit = min(16, size)
    inner = 2
    by_owner = first.reshape(depth, ctx, pieces, size)
    columns = [by_owner[:, :, k].reshape(depth, ctx * size) for k in range(pieces)]
    sums = (
        jnp.zeros((width, hidden), F32),
        jnp.zeros((width, hidden), F32),
        jnp.zeros((1, width), F32),
    )
    layer_pull = ()
    second_sum = jnp.zeros((tall, tall), F32)
    slopes, arrived, moved = [], [], []
    for k in range(pieces):
        gated, slope = first_mix(signal, columns[k].T, slab, k * size, ctx)
        slopes.append(slope)
        arrived.append(exchange(gated).reshape(ctx, size, rows, width))
    waits = ()
    scale = token_count ** (-0.5)
    gain_width = width // ctx
    for k in range(pieces):
        square = from_groups(squares(arrived[k], factor_turned, inner, waits))
        crosses = []
        for begin in range(0, size, unit):
            layer, pull, cross, *sums = mlp(
                arrived[k], (begin, unit), factor_turned, square, norm_gain, up, up_turned, down,
                down_turned, cotangent, k * size, sums, layer_pull, channels,
            )
            layer_pull = (layer, pull)
            crosses.append(cross)
        cross = from_groups(jnp.concatenate(crosses))
        waits = ()
        if k == pieces - 1:
            up_sum, down_sum, gain_sum = sums
            packed = jnp.concatenate(
                [
                    up_sum.reshape(ctx, gain_width * (hidden // tall), tall),
                    down_sum.T.reshape(ctx, hidden * width // (ctx * tall), tall),
                    jnp.pad(
                        gain_sum.reshape(ctx, 1, gain_width),
                        ((0, 0), (0, 15), (0, tall - gain_width)),
                    ),
                ],
                axis=1,
            )
            weights = Halving(packed, ctx, scale)
            waits = (weights.give,)
        back, second_sum = second(
            arrived[k], factor, factor_turned, square, cross, pull, cotangent, k * size,
            second_sum, channels, waits,
        )
        waits = (back,)
        if pieces > 1 and k == pieces - 1:
            back = hold(back, (weights.send(),))
            weights.keep((back,))
        moved.append(exchange(back.reshape(ctx * size, rows, width)))
    count = ctx * size
    own_rows, joint = tall // ctx, count == tall
    sums, firsts, gates, waits = (), [], [], ()
    factor_sorted = jnp.concatenate(columns, axis=1)
    if joint:
        above = ((0, 0), (pieces * (depth // ctx), 0), (0, 0))
        sums = (jnp.pad(second_sum.reshape(ctx, own_rows, tall).astype(BF16), above),)
    for k in range(pieces):
        if k == pieces - 1:
            packed = weights.finish(tuple(firsts))
            a = gain_width * (hidden // tall)
            b = a + hidden * width // (ctx * tall)
            grad_up = packed[:a].reshape(1, gain_width, hidden)
            grad_down = packed[a:b].reshape(1, hidden // ctx, width)
            grad_gain = packed[b, :gain_width][None]
            waits = (grad_up, grad_down, grad_gain, factor_sorted)
        first_grad, gate_grad, first_sum = gate(
            moved[k], signal, slopes[k], slab, k, pieces, sums, ctx, waits
        )
        sums = (first_sum,)
        firsts.append(first_grad)
        gates.append(gate_grad)
    parts = exchange(first_sum)
    grad_signal = signal_grad(
        factor_sorted, firsts, gates, tuple(k * size for k in range(pieces)), slab, ctx
    )
    grad_first, *rest = block_total(parts, pieces, ctx, scale, (grad_signal,))
    grad_second = (
        rest[0] if joint else Halving(second_sum.reshape(ctx, own_rows, tall), ctx, scale).finish()
    )
    return (
        layer,
        grad_signal,
        grad_first[None],
        grad_second[None],
        grad_up,
        grad_down,
        grad_gain,
    )


def solution(mesh):
    placed = (
        P("ctx", None, "ch"),
        P("ch", None, None),
        P("ch", None, None),
        P("ch", None, None),
        P("ch", None, None),
        P("ch", None),
        P("ctx", None, "ch"),
    )

    def layer(signal, factor_first, factor_second, up_weight, down_weight, norm_gain, cotangent):
        body = functools.partial(
            shards, mesh.shape["ctx"], signal.shape[2], signal.shape[0] * signal.shape[1]
        )
        return jax.shard_map(
            body,
            mesh=mesh,
            in_specs=placed,
            out_specs=(
                P("ctx", None, "ch"),
                P("ctx", None, "ch"),
                P("ch", "ctx", None),
                P("ch", "ctx", None),
                P("ch", "ctx", None),
                P("ch", "ctx", None),
                P("ch", "ctx"),
            ),
            check_vma=False,
        )(signal, factor_first, factor_second, up_weight, down_weight, norm_gain, cotangent)

    return layer
```

```python
import functools

import jax
import jax.numpy as jnp
from jax import lax
from jax.experimental import pallas as pl
from jax.experimental.pallas import tpu as pltpu
from jax.sharding import PartitionSpec as P

EPSILON = 1e-05
TANH_SCALE = 0.7978845608028654
TANH_CUBIC = 0.044715
BF16 = jnp.bfloat16
F32 = jnp.float32
MIB = 1024 * 1024


def sigmoid(values):
    return 0.5 * jnp.tanh(0.5 * values) + 0.5


def dot(left, right, left_dim, right_dim):
    return lax.dot_general(
        left, right, (((left_dim,), (right_dim,)), ((), ())), preferred_element_type=F32
    )


def to_row(column):
    return jnp.broadcast_to(column, (column.shape[0], 128)).T[0:1, :]


def to_column(row, width):
    spread = jnp.broadcast_to(row, (128, row.shape[1])).T
    return jnp.concatenate([spread] * (width // 128), axis=1)


def call(body, out_shape, cost, operands, in_specs, after=(), vmem=56, **options):
    flops, bytes_accessed = cost
    given, waits = len(operands), len(after)

    def ordered(*refs):
        body(*refs[:given], *refs[given + waits :])

    return pl.pallas_call(
        ordered,
        out_shape=out_shape,
        in_specs=[*in_specs, *([pl.BlockSpec(memory_space=pl.ANY)] * waits)],
        compiler_params=pltpu.CompilerParams(vmem_limit_bytes=vmem * MIB),
        cost_estimate=pl.CostEstimate(
            flops=int(flops), bytes_accessed=int(bytes_accessed), transcendentals=0
        ),
        **options,
    )(*operands, *after)


def whole(array):
    return pl.BlockSpec(array.shape, lambda s: (0,) * array.ndim)


def first_mix_body(slab, offset, ctx, signal_ref, factor_ref, gated_ref, slope_ref, turn):
    rows, depth, width = signal_ref.shape
    piece = gated_ref.shape[0] // ctx
    count = ctx * piece
    for a in range(rows):
        first = dot(factor_ref[...], signal_ref[a], 1, 0)
        own = jnp.concatenate(
            [signal_ref[a, d * slab + offset : d * slab + offset + piece, :] for d in range(ctx)],
            axis=0,
        )
        gate = sigmoid(own.astype(F32))
        gated = first * gate
        slope_ref[a] = (gated * (1.0 - gate)).astype(BF16)
        for lane in range(width // 128):
            turn[lane, pl.ds(a, count, stride=rows), :] = gated[:, lane * 128 : (lane + 1) * 128]
    for lane in range(width // 128):
        gated_ref[:, :, lane * 128 : (lane + 1) * 128] = (
            turn[lane].reshape(count, rows, 128).astype(BF16)
        )


def first_mix(signal, factor_turned, slab, offset, ctx, after=()):
    rows, depth, width = signal.shape
    count = factor_turned.shape[0]
    block = min(16, rows)
    return call(
        functools.partial(first_mix_body, slab, offset, ctx),
        (
            jax.ShapeDtypeStruct((count, rows, width), BF16),
            jax.ShapeDtypeStruct((rows, count, width), BF16),
        ),
        (2 * rows * depth * count * width, 2 * rows * width * (depth + 2 * count)),
        (signal, factor_turned),
        [
            pl.BlockSpec((block, depth, width), lambda s: (s, 0, 0)),
            pl.BlockSpec((count, depth), lambda s: (0, 0)),
        ],
        after,
        grid=(rows // block,),
        out_specs=(
            pl.BlockSpec((count, block, width), lambda s: (0, s, 0)),
            pl.BlockSpec((block, count, width), lambda s: (s, 0, 0)),
        ),
        scratch_shapes=[pltpu.VMEM((width // 128, count * block, 128), F32)],
        name="first_mix",
    )


def tokens_of(gated_ref, t):
    ctx, _, rows, width = gated_ref.shape
    return gated_ref[:, t].reshape(ctx * rows, width)


def square_body(gated_ref, factor_ref, square_ref):
    steps, inner, _ = square_ref.shape
    for t in range(steps * inner):
        mixed = dot(factor_ref[...], tokens_of(gated_ref, t), 1, 0)
        square_ref[t // inner, t % inner : t % inner + 1, :] = to_row(
            jnp.sum(mixed * mixed, axis=1, keepdims=True)
        )


def squares(gated, factor_turned, inner, after=()):
    ctx, piece, rows, width = gated.shape
    tall = factor_turned.shape[0]
    block = min(8, piece)
    return call(
        square_body,
        jax.ShapeDtypeStruct((piece // inner, inner, tall), F32),
        (2 * piece * tall * tall * width, 2 * gated.size),
        (gated, factor_turned),
        [
            pl.BlockSpec((ctx, block, rows, width), lambda s: (0, s, 0, 0)),
            whole(factor_turned),
        ],
        after,
        grid=(piece // block,),
        out_specs=pl.BlockSpec((block // inner, inner, tall), lambda s: (s, 0, 0)),
        name="squares",
    )


def gathered(parts_ref, step, t):
    return sum(parts_ref[g, step, t : t + 1, :] for g in range(parts_ref.shape[0]))


def inverse_of(square_ref, step, t, channels):
    return lax.rsqrt(gathered(square_ref, step, t) * (1.0 / channels) + EPSILON)


def mlp_body(
    channels, carried, gated_ref, factor_ref, square_ref, gain_ref, up_ref, up_turned_ref,
    down_ref, down_turned_ref, cotangent_ref, up_in_ref, down_in_ref, gain_in_ref, *refs,
):
    (layer_ref, pull_ref, cross_ref, up_out_ref, down_out_ref, gain_out_ref,
     mixed_all, normed_all, act_all, pre_all, spread_all) = refs[carried:]
    inner = square_ref.shape[2]
    tall = factor_ref.shape[0]
    width = gain_ref.shape[1]
    hidden = up_ref.shape[1]

    @pl.when(pl.program_id(0) == 0)
    def _():
        up_out_ref[...] = up_in_ref[...]
        down_out_ref[...] = down_in_ref[...]
        gain_out_ref[...] = gain_in_ref[...]

    for t in range(inner):
        inverse = inverse_of(square_ref, 0, t, channels)
        part = slice(t * tall, (t + 1) * tall)
        mixed = dot(factor_ref[...], tokens_of(gated_ref, t), 1, 0)
        spread = to_column(inverse, width)
        mixed_all[part, :] = mixed
        spread_all[part, :] = spread
        normed_all[part, :] = (mixed * spread * gain_ref[...]).astype(BF16)
    upstream = cotangent_ref[...].reshape(inner * tall, width)
    normed = normed_all[...]
    step = min(256, hidden)
    for h in range(0, hidden, step):
        part = slice(h, h + step)
        pre = dot(normed, up_ref[:, part], 1, 0)
        back = dot(upstream, down_turned_ref[:, part], 1, 0)
        square = pre * pre
        lean = jnp.tanh(pre * (square * (TANH_SCALE * TANH_CUBIC) + TANH_SCALE))
        half = 0.5 * lean + 0.5
        act = pre * half
        act_all[:, part] = act.astype(BF16)
        bend = square * (6.0 * TANH_SCALE * TANH_CUBIC) + 2.0 * TANH_SCALE
        pre_all[:, part] = (back * (half + act * (1.0 - half) * bend)).astype(BF16)
    mixed = mixed_all[...]
    layer = mixed + dot(act_all[...], down_ref[...], 1, 0)
    layer_ref[...] = layer.astype(BF16).reshape(layer_ref.shape)
    down_out_ref[...] += dot(upstream, act_all[...], 0, 0)
    up_out_ref[...] += dot(normed, pre_all[...], 0, 0)
    grad_normed = dot(pre_all[...], up_turned_ref[...], 1, 0)
    spread = spread_all[...]
    gain = gain_ref[...]
    weighed = grad_normed * mixed
    gain_out_ref[...] += jnp.sum(weighed * spread, axis=0, keepdims=True)
    cross = jnp.sum(weighed * gain, axis=1, keepdims=True)
    for t in range(inner):
        cross_ref[0, t : t + 1, :] = to_row(cross[t * tall : (t + 1) * tall])
    pull_ref[...] = (grad_normed * gain * spread).astype(BF16).reshape(pull_ref.shape)


def mlp(gated, part, factor_turned, square, gain, up, up_turned, down, down_turned, cotangent,
        first_piece, sums, layer_pull, channels, after=()):
    ctx, _, rows, width = gated.shape
    groups, _, inner, tall = square.shape
    hidden = up.shape[1]
    begin, piece = part
    steps, skip = piece // inner, begin // inner
    start = (first_piece + begin) // inner
    tokens = inner * tall
    by_token = pl.BlockSpec((inner, tall, width), lambda s: (s + start, 0, 0))
    stays = pl.BlockSpec(memory_space=pl.ANY)
    full = jax.ShapeDtypeStruct(cotangent.shape, BF16)
    carried = len(layer_pull)
    aliases = {9: 3, 10: 4, 11: 5}
    for i in range(carried):
        aliases[12 + i] = i
    return call(
        functools.partial(mlp_body, channels, carried),
        (
            full,
            full,
            jax.ShapeDtypeStruct((steps, inner, tall), F32),
            *(jax.ShapeDtypeStruct(array.shape, F32) for array in sums),
        ),
        (12 * piece * tall * width * hidden, 8 * piece * tall * width),
        (gated, factor_turned, square, gain, up, up_turned, down, down_turned, cotangent, *sums,
         *layer_pull),
        [
            pl.BlockSpec((ctx, inner, rows, width), lambda s: (0, s + skip, 0, 0)),
            whole(factor_turned),
            pl.BlockSpec((groups, 1, inner, tall), lambda s: (0, s + skip, 0, 0)),
            whole(gain), whole(up), whole(up_turned), whole(down), whole(down_turned),
            by_token,
            *(whole(array) for array in sums),
            *([stays] * carried),
        ],
        after,
        grid=(steps,),
        out_specs=(
            by_token, by_token,
            pl.BlockSpec((1, inner, tall), lambda s: (s, 0, 0)),
            *(whole(array) for array in sums),
        ),
        scratch_shapes=[
            pltpu.VMEM((tokens, width), F32),
            pltpu.VMEM((tokens, width), BF16),
            pltpu.VMEM((tokens, hidden), BF16),
            pltpu.VMEM((tokens, hidden), BF16),
            pltpu.VMEM((tokens, width), F32),
        ],
        input_output_aliases=aliases,
        name="mlp",
    )


def second_body(
    channels, gated_ref, factor_ref, factor_turned_ref, square_ref, cross_ref, pull_ref,
    cotangent_ref, sum_in_ref, moved_ref, sum_out_ref,
):
    _, steps, inner, tall = square_ref.shape
    ctx, _, rows, width = gated_ref.shape

    @pl.when(pl.program_id(0) == 0)
    def _():
        sum_out_ref[...] = sum_in_ref[...]

    total = sum_out_ref[...]
    for t in range(steps * inner):
        gated = tokens_of(gated_ref, t)
        mixed = dot(factor_turned_ref[...], gated, 1, 0)
        inverse = inverse_of(square_ref, t // inner, t % inner, channels)
        cross = gathered(cross_ref, t // inner, t % inner)
        weight = to_column(inverse * inverse * inverse * cross * (1.0 / channels), width)
        grad = (
            cotangent_ref[t].astype(F32) + pull_ref[t].astype(F32) - mixed * weight
        ).astype(BF16)
        total += dot(gated, grad, 1, 1)
        moved_ref[:, t] = dot(factor_ref[...], grad, 1, 0).astype(BF16).reshape(ctx, rows, width)
    sum_out_ref[...] = total


def second(gated, factor, factor_turned, square, cross, pull, cotangent, first_piece, total,
           channels, after=()):
    ctx, piece, rows, width = gated.shape
    groups, steps, inner, tall = square.shape
    block = max(size for size in (4, 2, 1) if steps % size == 0)
    count = block * inner
    start = first_piece // count
    by_piece = pl.BlockSpec((groups, block, inner, tall), lambda s: (0, s, 0, 0))
    by_token = pl.BlockSpec((count, tall, width), lambda s: (s + start, 0, 0))
    return call(
        functools.partial(second_body, channels),
        (
            jax.ShapeDtypeStruct(gated.shape, BF16),
            jax.ShapeDtypeStruct(total.shape, F32),
        ),
        (6 * piece * tall * tall * width, 8 * gated.size),
        (gated, factor, factor_turned, square, cross, pull, cotangent, total),
        [
            pl.BlockSpec((ctx, count, rows, width), lambda s: (0, s, 0, 0)),
            whole(factor), whole(factor_turned), by_piece, by_piece, by_token, by_token,
            whole(total),
        ],
        after,
        grid=(steps // block,),
        out_specs=(
            pl.BlockSpec((ctx, count, rows, width), lambda s: (0, s, 0, 0)),
            whole(total),
        ),
        input_output_aliases={7: 1},
        name="second",
    )


def gate_body(slab, offset, ctx, carried, moved_ref, signal_ref, slope_ref, *refs):
    first_ref, gate_ref, sum_ref, turn, total_ref = refs[carried:]
    rows, depth, width = signal_ref.shape
    count = moved_ref.shape[0]
    piece = count // ctx

    @pl.when(pl.program_id(0) == 0)
    def _():
        total_ref[...] = jnp.zeros_like(total_ref)

    for lane in range(width // 128):
        turn[lane] = (
            moved_ref[:, :, lane * 128 : (lane + 1) * 128]
            .astype(F32)
            .reshape(count * rows, 128)
        )
    total = total_ref[...]
    for a in range(rows):
        grad = jnp.concatenate(
            [turn[lane, pl.ds(a, count, stride=rows), :] for lane in range(width // 128)], axis=1
        )
        own = jnp.concatenate(
            [signal_ref[a, d * slab + offset : d * slab + offset + piece, :] for d in range(ctx)],
            axis=0,
        )
        first = (grad * sigmoid(own.astype(F32))).astype(BF16)
        first_ref[a] = first
        gate_ref[a] = (grad * slope_ref[a].astype(F32)).astype(BF16)
        total += dot(signal_ref[a], first, 1, 1)
    total_ref[...] = total

    @pl.when(pl.program_id(0) == pl.num_programs(0) - 1)
    def _():
        sum_ref[...] = total_ref[...].astype(BF16).reshape(sum_ref.shape)


def gate(moved, signal, slope, slab, k, pieces, sums, ctx, after=()):
    rows, depth, width = signal.shape
    count = moved.shape[0]
    block = min(16, rows)
    by_row = pl.BlockSpec((block, count, width), lambda s: (s, 0, 0))
    return call(
        functools.partial(gate_body, slab, k * (count // ctx), ctx, len(sums)),
        (
            jax.ShapeDtypeStruct((rows, count, width), BF16),
            jax.ShapeDtypeStruct((rows, count, width), BF16),
            jax.ShapeDtypeStruct(sums[0].shape, BF16)
            if sums
            else jax.ShapeDtypeStruct((ctx, pieces * (depth // ctx), count), BF16),
        ),
        (2 * rows * depth * count * width, 2 * rows * width * (depth + 4 * count)),
        (moved, signal, slope, *sums),
        [
            pl.BlockSpec((count, block, width), lambda s: (0, s, 0)),
            pl.BlockSpec((block, depth, width), lambda s: (s, 0, 0)),
            by_row,
            *([pl.BlockSpec(memory_space=pl.ANY)] * len(sums)),
        ],
        after,
        grid=(rows // block,),
        out_specs=(
            by_row,
            by_row,
            pl.BlockSpec((ctx, depth // ctx, count), lambda s: (0, k, 0)),
        ),
        scratch_shapes=[
            pltpu.VMEM((width // 128, count * block, 128), F32),
            pltpu.VMEM((depth, count), F32),
        ],
        input_output_aliases={3: 2} if sums else {},
        name="gate",
    )


def signal_body(offsets, slab, ctx, factor_ref, *refs):
    pieces = len(offsets)
    firsts, gates, out_ref = refs[:pieces], refs[pieces : 2 * pieces], refs[-1]
    for a in range(out_ref.shape[0]):
        grads = jnp.concatenate([first[a] for first in firsts], axis=0)
        total = dot(factor_ref[...], grads, 1, 0)
        for gate_ref, offset in zip(gates, offsets):
            piece = gate_ref.shape[1] // ctx
            for d in range(ctx):
                place = slice(d * slab + offset, d * slab + offset + piece)
                out_ref[a, place, :] = (
                    total[place] + gate_ref[a, d * piece : (d + 1) * piece, :].astype(F32)
                ).astype(BF16)


def signal_grad(factor, firsts, gates, offsets, slab, ctx, after=()):
    rows, _, width = firsts[0].shape
    depth = factor.shape[0]
    block = min(8, rows)
    by_row = [pl.BlockSpec((block, *array.shape[1:]), lambda s: (s, 0, 0)) for array in firsts]
    return call(
        functools.partial(signal_body, offsets, slab, ctx),
        jax.ShapeDtypeStruct((rows, depth, width), BF16),
        (2 * rows * depth * depth * width, 6 * rows * depth * width),
        (factor, *firsts, *gates),
        [whole(factor), *by_row, *by_row],
        after,
        grid=(rows // block,),
        out_specs=pl.BlockSpec((block, depth, width), lambda s: (s, 0, 0)),
        name="signal_grad",
    )


def fold_body(scale, mine_ref, values_ref, got_ref, *refs):
    del mine_ref
    total = values_ref[...].reshape(refs[-1].shape) + got_ref[...].astype(F32)
    refs[-1][...] = total * scale


def fold(values, got, mine, scale, after=()):
    blocks, _, rows, columns = values.shape
    return pl.pallas_call(
        functools.partial(fold_body, scale),
        out_shape=jax.ShapeDtypeStruct((blocks, rows, columns), F32),
        grid_spec=pltpu.PrefetchScalarGridSpec(
            num_scalar_prefetch=1,
            grid=(blocks,),
            in_specs=[
                pl.BlockSpec((1, 1, rows, columns), lambda s, mine: (s, mine[0], 0, 0)),
                pl.BlockSpec((1, rows, columns), lambda s, mine: (s, 0, 0)),
                *([pl.BlockSpec(memory_space=pl.ANY)] * len(after)),
            ],
            out_specs=pl.BlockSpec((1, rows, columns), lambda s, mine: (s, 0, 0)),
        ),
        compiler_params=pltpu.CompilerParams(vmem_limit_bytes=56 * MIB),
        cost_estimate=pl.CostEstimate(
            flops=got.size, bytes_accessed=10 * got.size, transcendentals=0
        ),
        name="fold",
    )(mine.reshape(1), values, got, *after)


def finish_body(scale, mine_ref, values_ref, got_ref, *refs):
    del mine_ref
    up_ref, down_ref, gain_ref = refs[-3:]
    total = (values_ref[0, 0] + got_ref[0].astype(F32)) * scale
    rows, width = up_ref.shape[0], total.shape[1]
    start = 0
    for lane in range(0, up_ref.shape[1], width):
        up_ref[:, lane : lane + width] = total[start : start + rows]
        start += rows
    down_ref[...] = total[start : start + down_ref.shape[0]]
    start += down_ref.shape[0]
    gain_ref[...] = total[start : start + 1, : gain_ref.shape[1]]


def finish_weights(values, got, mine, shapes, scale, after):
    _, _, rows, columns = values.shape
    return pl.pallas_call(
        functools.partial(finish_body, scale),
        out_shape=tuple(jax.ShapeDtypeStruct(shape, F32) for shape in shapes),
        grid_spec=pltpu.PrefetchScalarGridSpec(
            num_scalar_prefetch=1,
            grid=(1,),
            in_specs=[
                pl.BlockSpec((1, 1, rows, columns), lambda s, mine: (0, mine[0], 0, 0)),
                pl.BlockSpec((1, rows, columns), lambda s, mine: (0, 0, 0)),
                *([pl.BlockSpec(memory_space=pl.ANY)] * len(after)),
            ],
            out_specs=tuple(pl.BlockSpec(shape, lambda s, mine: (0, 0)) for shape in shapes),
        ),
        compiler_params=pltpu.CompilerParams(vmem_limit_bytes=56 * MIB),
        cost_estimate=pl.CostEstimate(
            flops=got.size, bytes_accessed=10 * got.size, transcendentals=0
        ),
        name="finish_weights",
    )(mine.reshape(1), values, got, *after)


class Halving:
    def __init__(self, values, ctx, scale):
        self.ctx, self.bit, self.scale = ctx, 1, scale
        self.values = values
        self.halve()

    def halve(self):
        self.halves = self.values.reshape((-1, 2) + self.values.shape[1:])
        self.mine = (lax.axis_index("ctx") // self.bit) % 2
        self.give = lax.dynamic_index_in_dim(
            self.halves, 1 - self.mine, 1, keepdims=False
        ).astype(BF16)

    def send(self):
        bit = self.bit
        self.got = lax.ppermute(self.give, "ctx", [(i, i ^ bit) for i in range(self.ctx)])
        return self.got

    def keep(self, after=()):
        self.bit = 2 * self.bit
        scale = 1.0 if self.bit < self.ctx else self.scale
        self.values = fold(self.halves, self.got, self.mine, scale, after)
        if self.bit < self.ctx:
            self.halve()

    def finish(self, after=()):
        while self.bit < self.ctx:
            self.send()
            self.keep(after)
        return self.values[0]


def block_total_body(pieces, ctx, scale, parts_ref, first_ref, *rest):
    rows = first_ref.shape[0]
    count = parts_ref.shape[2]
    size = count // ctx

    def total_of(start, stop):
        total = parts_ref[0, start:stop].astype(F32)
        for source in range(1, ctx):
            total += parts_ref[source, start:stop].astype(F32)
        return total * scale

    for k in range(pieces):
        total = total_of(k * rows, (k + 1) * rows)
        for d in range(ctx):
            place = (d * pieces + k) * size
            first_ref[:, place : place + size] = total[:, d * size : (d + 1) * size]
    if rest:
        rest[0][...] = total_of(pieces * rows, parts_ref.shape[1])


def block_total(parts, pieces, ctx, scale, after=()):
    _, all_rows, count = parts.shape
    depth = pieces * count
    more = all_rows - pieces * (depth // ctx)
    shapes = [jax.ShapeDtypeStruct((depth // ctx, depth), F32)]
    if more:
        shapes.append(jax.ShapeDtypeStruct((more, count), F32))
    return call(
        functools.partial(block_total_body, pieces, ctx, scale),
        tuple(shapes),
        (parts.size, 4 * parts.size),
        (parts,),
        [whole(parts)],
        after,
        grid=(1,),
        out_specs=tuple(pl.BlockSpec(shape.shape, lambda s: (0, 0)) for shape in shapes),
        name="block_total",
    )


def hold(array, after):
    return pl.pallas_call(
        lambda *refs: None,
        out_shape=jax.ShapeDtypeStruct(array.shape, array.dtype),
        in_specs=[pl.BlockSpec(memory_space=pl.ANY)] * (1 + len(after)),
        out_specs=pl.BlockSpec(memory_space=pl.ANY),
        input_output_aliases={0: 0},
        compiler_params=pltpu.CompilerParams(vmem_limit_bytes=56 * MIB),
        name="hold",
    )(array, *after)


def from_groups(partial_value):
    return lax.all_gather(partial_value, "ch")


def exchange(block):
    return lax.all_to_all(block, "ctx", split_axis=0, concat_axis=0, tiled=True)


def shards(ctx, channels, token_count, signal, factor_first, factor_second, up_weight,
           down_weight, norm_gain, cotangent):
    rows, depth, width = signal.shape
    slab, tall, _ = cotangent.shape
    first, factor = factor_first[0], factor_second[0]
    up, down = up_weight[0], down_weight[0]
    hidden = up.shape[1]
    factor_turned, up_turned, down_turned = factor.T, up.T, down.T
    pieces = 2 if slab % 32 == 0 else 1
    size = slab // pieces
    unit = min(16, size)
    inner = 2
    by_owner = first.reshape(depth, ctx, pieces, size)
    columns = [by_owner[:, :, k].reshape(depth, ctx * size) for k in range(pieces)]
    sums = (
        jnp.zeros((width, hidden), F32),
        jnp.zeros((width, hidden), F32),
        jnp.zeros((1, width), F32),
    )
    layer_pull = ()
    second_sum = jnp.zeros((tall, tall), F32)
    slopes, arrived, moved = [], [], []
    for k in range(pieces):
        gated, slope = first_mix(signal, columns[k].T, slab, k * size, ctx)
        slopes.append(slope)
        arrived.append(exchange(gated).reshape(ctx, size, rows, width))
    waits = ()
    scale = token_count ** (-0.5)
    gain_width = width // ctx
    for k in range(pieces):
        square = from_groups(squares(arrived[k], factor_turned, inner, waits))
        crosses = []
        for begin in range(0, size, unit):
            layer, pull, cross, *sums = mlp(
                arrived[k], (begin, unit), factor_turned, square, norm_gain, up, up_turned, down,
                down_turned, cotangent, k * size, sums, layer_pull, channels,
            )
            layer_pull = (layer, pull)
            crosses.append(cross)
        cross = from_groups(jnp.concatenate(crosses))
        waits = ()
        if k == pieces - 1:
            up_sum, down_sum, gain_sum = sums
            packed = jnp.concatenate(
                [
                    up_sum.reshape(ctx, gain_width, hidden // width, width)
                    .transpose(0, 2, 1, 3)
                    .reshape(ctx, hidden // ctx, width),
                    down_sum.T.reshape(ctx, hidden // ctx, width),
                    jnp.pad(
                        gain_sum.reshape(ctx, 1, gain_width),
                        ((0, 0), (0, 15), (0, width - gain_width)),
                    ),
                ],
                axis=1,
            )
            weights = Halving(packed, ctx, scale)
            waits = (weights.give,)
        back, second_sum = second(
            arrived[k], factor, factor_turned, square, cross, pull, cotangent, k * size,
            second_sum, channels, waits,
        )
        waits = (back,)
        if pieces > 1 and k == pieces - 1:
            back = hold(back, (weights.send(),))
            weights.keep((back,))
        moved.append(exchange(back.reshape(ctx * size, rows, width)))
    count = ctx * size
    own_rows, joint = tall // ctx, count == tall
    sums, firsts, gates, waits = (), [], [], ()
    factor_sorted = jnp.concatenate(columns, axis=1)
    if joint:
        above = ((0, 0), (pieces * (depth // ctx), 0), (0, 0))
        sums = (jnp.pad(second_sum.reshape(ctx, own_rows, tall).astype(BF16), above),)
    for k in range(pieces):
        if k == pieces - 1:
            while 2 * weights.bit < ctx:
                weights.send()
                weights.keep(tuple(firsts))
            waits = (weights.give, factor_sorted)
        first_grad, gate_grad, first_sum = gate(
            moved[k], signal, slopes[k], slab, k, pieces, sums, ctx, waits
        )
        sums = (first_sum,)
        firsts.append(first_grad)
        gates.append(gate_grad)
    parts = exchange(first_sum)
    grad_signal = signal_grad(
        factor_sorted, firsts, gates, tuple(k * size for k in range(pieces)), slab, ctx
    )
    grad_up, grad_down, grad_gain = finish_weights(
        weights.halves, weights.send(), weights.mine,
        ((gain_width, hidden), (hidden // ctx, width), (1, gain_width)), scale, (grad_signal,),
    )
    grad_first, *rest = block_total(parts, pieces, ctx, scale, (grad_signal, grad_gain))
    grad_second = (
        rest[0] if joint else Halving(second_sum.reshape(ctx, own_rows, tall), ctx, scale).finish()
    )
    return (
        layer,
        grad_signal,
        grad_first[None],
        grad_second[None],
        grad_up[None],
        grad_down[None],
        grad_gain,
    )


def solution(mesh):
    placed = (
        P("ctx", None, "ch"),
        P("ch", None, None),
        P("ch", None, None),
        P("ch", None, None),
        P("ch", None, None),
        P("ch", None),
        P("ctx", None, "ch"),
    )

    def layer(signal, factor_first, factor_second, up_weight, down_weight, norm_gain, cotangent):
        body = functools.partial(
            shards, mesh.shape["ctx"], signal.shape[2], signal.shape[0] * signal.shape[1]
        )
        return jax.shard_map(
            body,
            mesh=mesh,
            in_specs=placed,
            out_specs=(
                P("ctx", None, "ch"),
                P("ctx", None, "ch"),
                P("ch", "ctx", None),
                P("ch", "ctx", None),
                P("ch", "ctx", None),
                P("ch", "ctx", None),
                P("ch", "ctx"),
            ),
            check_vma=False,
        )(signal, factor_first, factor_second, up_weight, down_weight, norm_gain, cotangent)

    return layer
```

```python
import functools

import jax
import jax.numpy as jnp
from jax import lax
from jax.experimental import pallas as pl
from jax.experimental.pallas import tpu as pltpu
from jax.sharding import PartitionSpec as P

EPSILON = 1e-05
TANH_SCALE = 0.7978845608028654
TANH_CUBIC = 0.044715
BF16 = jnp.bfloat16
F32 = jnp.float32
MIB = 1024 * 1024


def sigmoid(values):
    return 0.5 * jnp.tanh(0.5 * values) + 0.5


def dot(left, right, left_dim, right_dim):
    return lax.dot_general(
        left, right, (((left_dim,), (right_dim,)), ((), ())), preferred_element_type=F32
    )


def to_row(column):
    return jnp.broadcast_to(column, (column.shape[0], 128)).T[0:1, :]


def to_column(row, width):
    spread = jnp.broadcast_to(row, (128, row.shape[1])).T
    return jnp.concatenate([spread] * (width // 128), axis=1)


def call(body, out_shape, cost, operands, in_specs, after=(), vmem=56, **options):
    flops, bytes_accessed = cost
    given, waits = len(operands), len(after)

    def ordered(*refs):
        body(*refs[:given], *refs[given + waits :])

    return pl.pallas_call(
        ordered,
        out_shape=out_shape,
        in_specs=[*in_specs, *([pl.BlockSpec(memory_space=pl.ANY)] * waits)],
        compiler_params=pltpu.CompilerParams(vmem_limit_bytes=vmem * MIB),
        cost_estimate=pl.CostEstimate(
            flops=int(flops), bytes_accessed=int(bytes_accessed), transcendentals=0
        ),
        **options,
    )(*operands, *after)


def whole(array):
    return pl.BlockSpec(array.shape, lambda s: (0,) * array.ndim)


def first_mix_body(slab, offset, ctx, signal_ref, factor_ref, gated_ref, slope_ref, turn):
    rows, depth, width = signal_ref.shape
    piece = gated_ref.shape[0] // ctx
    count = ctx * piece
    for a in range(rows):
        first = dot(factor_ref[...], signal_ref[a], 1, 0)
        own = jnp.concatenate(
            [signal_ref[a, d * slab + offset : d * slab + offset + piece, :] for d in range(ctx)],
            axis=0,
        )
        gate = sigmoid(own.astype(F32))
        gated = first * gate
        slope_ref[a] = (gated * (1.0 - gate)).astype(BF16)
        for lane in range(width // 128):
            turn[lane, pl.ds(a, count, stride=rows), :] = gated[:, lane * 128 : (lane + 1) * 128]
    for lane in range(width // 128):
        gated_ref[:, :, lane * 128 : (lane + 1) * 128] = (
            turn[lane].reshape(count, rows, 128).astype(BF16)
        )


def first_mix(signal, factor_turned, slab, offset, ctx, after=()):
    rows, depth, width = signal.shape
    count = factor_turned.shape[0]
    block = min(16, rows)
    return call(
        functools.partial(first_mix_body, slab, offset, ctx),
        (
            jax.ShapeDtypeStruct((count, rows, width), BF16),
            jax.ShapeDtypeStruct((rows, count, width), BF16),
        ),
        (2 * rows * depth * count * width, 2 * rows * width * (depth + 2 * count)),
        (signal, factor_turned),
        [
            pl.BlockSpec((block, depth, width), lambda s: (s, 0, 0)),
            pl.BlockSpec((count, depth), lambda s: (0, 0)),
        ],
        after,
        grid=(rows // block,),
        out_specs=(
            pl.BlockSpec((count, block, width), lambda s: (0, s, 0)),
            pl.BlockSpec((block, count, width), lambda s: (s, 0, 0)),
        ),
        scratch_shapes=[pltpu.VMEM((width // 128, count * block, 128), F32)],
        name="first_mix",
    )


def tokens_of(gated_ref, t):
    ctx, _, rows, width = gated_ref.shape
    return gated_ref[:, t].reshape(ctx * rows, width)


def square_body(gated_ref, factor_ref, square_ref):
    steps, inner, _ = square_ref.shape
    for t in range(steps * inner):
        mixed = dot(factor_ref[...], tokens_of(gated_ref, t), 1, 0)
        square_ref[t // inner, t % inner : t % inner + 1, :] = to_row(
            jnp.sum(mixed * mixed, axis=1, keepdims=True)
        )


def squares(gated, factor_turned, inner, after=()):
    ctx, piece, rows, width = gated.shape
    tall = factor_turned.shape[0]
    block = min(8, piece)
    return call(
        square_body,
        jax.ShapeDtypeStruct((piece // inner, inner, tall), F32),
        (2 * piece * tall * tall * width, 2 * gated.size),
        (gated, factor_turned),
        [
            pl.BlockSpec((ctx, block, rows, width), lambda s: (0, s, 0, 0)),
            whole(factor_turned),
        ],
        after,
        grid=(piece // block,),
        out_specs=pl.BlockSpec((block // inner, inner, tall), lambda s: (s, 0, 0)),
        name="squares",
    )


def gathered(parts_ref, step, t):
    return sum(parts_ref[g, step, t : t + 1, :] for g in range(parts_ref.shape[0]))


def inverse_of(square_ref, step, t, channels):
    return lax.rsqrt(gathered(square_ref, step, t) * (1.0 / channels) + EPSILON)


def mlp_body(
    channels, carried, gated_ref, factor_ref, square_ref, gain_ref, up_ref, up_turned_ref,
    down_ref, down_turned_ref, cotangent_ref, up_in_ref, down_in_ref, gain_in_ref, *refs,
):
    (layer_ref, pull_ref, cross_ref, up_out_ref, down_out_ref, gain_out_ref,
     mixed_all, normed_all, act_all, pre_all, spread_all) = refs[carried:]
    inner = square_ref.shape[2]
    tall = factor_ref.shape[0]
    width = gain_ref.shape[1]
    hidden = up_ref.shape[1]

    @pl.when(pl.program_id(0) == 0)
    def _():
        up_out_ref[...] = up_in_ref[...]
        down_out_ref[...] = down_in_ref[...]
        gain_out_ref[...] = gain_in_ref[...]

    for t in range(inner):
        inverse = inverse_of(square_ref, 0, t, channels)
        part = slice(t * tall, (t + 1) * tall)
        mixed = dot(factor_ref[...], tokens_of(gated_ref, t), 1, 0)
        spread = to_column(inverse, width)
        mixed_all[part, :] = mixed
        spread_all[part, :] = spread
        normed_all[part, :] = (mixed * spread * gain_ref[...]).astype(BF16)
    upstream = cotangent_ref[...].reshape(inner * tall, width)
    normed = normed_all[...]
    step = min(256, hidden)
    for h in range(0, hidden, step):
        part = slice(h, h + step)
        pre = dot(normed, up_ref[:, part], 1, 0)
        back = dot(upstream, down_turned_ref[:, part], 1, 0)
        square = pre * pre
        lean = jnp.tanh(pre * (square * (TANH_SCALE * TANH_CUBIC) + TANH_SCALE))
        half = 0.5 * lean + 0.5
        act = pre * half
        act_all[:, part] = act.astype(BF16)
        bend = square * (6.0 * TANH_SCALE * TANH_CUBIC) + 2.0 * TANH_SCALE
        pre_all[:, part] = (back * (half + act * (1.0 - half) * bend)).astype(BF16)
    mixed = mixed_all[...]
    layer = mixed + dot(act_all[...], down_ref[...], 1, 0)
    layer_ref[...] = layer.astype(BF16).reshape(layer_ref.shape)
    down_out_ref[...] += dot(upstream, act_all[...], 0, 0)
    up_out_ref[...] += dot(normed, pre_all[...], 0, 0)
    grad_normed = dot(pre_all[...], up_turned_ref[...], 1, 0)
    spread = spread_all[...]
    gain = gain_ref[...]
    weighed = grad_normed * mixed
    gain_out_ref[...] += jnp.sum(weighed * spread, axis=0, keepdims=True)
    cross = jnp.sum(weighed * gain, axis=1, keepdims=True)
    for t in range(inner):
        cross_ref[0, t : t + 1, :] = to_row(cross[t * tall : (t + 1) * tall])
    pull_ref[...] = (grad_normed * gain * spread).astype(BF16).reshape(pull_ref.shape)


def mlp(gated, part, factor_turned, square, gain, up, up_turned, down, down_turned, cotangent,
        first_piece, sums, layer_pull, channels, after=()):
    ctx, _, rows, width = gated.shape
    groups, _, inner, tall = square.shape
    hidden = up.shape[1]
    begin, piece = part
    steps, skip = piece // inner, begin // inner
    start = (first_piece + begin) // inner
    tokens = inner * tall
    by_token = pl.BlockSpec((inner, tall, width), lambda s: (s + start, 0, 0))
    stays = pl.BlockSpec(memory_space=pl.ANY)
    full = jax.ShapeDtypeStruct(cotangent.shape, BF16)
    carried = len(layer_pull)
    aliases = {9: 3, 10: 4, 11: 5}
    for i in range(carried):
        aliases[12 + i] = i
    return call(
        functools.partial(mlp_body, channels, carried),
        (
            full,
            full,
            jax.ShapeDtypeStruct((steps, inner, tall), F32),
            *(jax.ShapeDtypeStruct(array.shape, F32) for array in sums),
        ),
        (12 * piece * tall * width * hidden, 8 * piece * tall * width),
        (gated, factor_turned, square, gain, up, up_turned, down, down_turned, cotangent, *sums,
         *layer_pull),
        [
            pl.BlockSpec((ctx, inner, rows, width), lambda s: (0, s + skip, 0, 0)),
            whole(factor_turned),
            pl.BlockSpec((groups, 1, inner, tall), lambda s: (0, s + skip, 0, 0)),
            whole(gain), whole(up), whole(up_turned), whole(down), whole(down_turned),
            by_token,
            *(whole(array) for array in sums),
            *([stays] * carried),
        ],
        after,
        grid=(steps,),
        out_specs=(
            by_token, by_token,
            pl.BlockSpec((1, inner, tall), lambda s: (s, 0, 0)),
            *(whole(array) for array in sums),
        ),
        scratch_shapes=[
            pltpu.VMEM((tokens, width), F32),
            pltpu.VMEM((tokens, width), BF16),
            pltpu.VMEM((tokens, hidden), BF16),
            pltpu.VMEM((tokens, hidden), BF16),
            pltpu.VMEM((tokens, width), F32),
        ],
        input_output_aliases=aliases,
        name="mlp",
    )


def second_body(
    channels, gated_ref, factor_ref, factor_turned_ref, square_ref, cross_ref, pull_ref,
    cotangent_ref, sum_in_ref, moved_ref, sum_out_ref,
):
    _, steps, inner, tall = square_ref.shape
    ctx, _, rows, width = gated_ref.shape

    @pl.when(pl.program_id(0) == 0)
    def _():
        sum_out_ref[...] = sum_in_ref[...]

    total = sum_out_ref[...]
    for t in range(steps * inner):
        gated = tokens_of(gated_ref, t)
        mixed = dot(factor_turned_ref[...], gated, 1, 0)
        inverse = inverse_of(square_ref, t // inner, t % inner, channels)
        cross = gathered(cross_ref, t // inner, t % inner)
        weight = to_column(inverse * inverse * inverse * cross * (1.0 / channels), width)
        grad = (
            cotangent_ref[t].astype(F32) + pull_ref[t].astype(F32) - mixed * weight
        ).astype(BF16)
        total += dot(gated, grad, 1, 1)
        moved_ref[:, t] = dot(factor_ref[...], grad, 1, 0).astype(BF16).reshape(ctx, rows, width)
    sum_out_ref[...] = total


def second(gated, factor, factor_turned, square, cross, pull, cotangent, first_piece, total,
           channels, after=()):
    ctx, piece, rows, width = gated.shape
    groups, steps, inner, tall = square.shape
    block = max(size for size in (4, 2, 1) if steps % size == 0)
    count = block * inner
    start = first_piece // count
    by_piece = pl.BlockSpec((groups, block, inner, tall), lambda s: (0, s, 0, 0))
    by_token = pl.BlockSpec((count, tall, width), lambda s: (s + start, 0, 0))
    return call(
        functools.partial(second_body, channels),
        (
            jax.ShapeDtypeStruct(gated.shape, BF16),
            jax.ShapeDtypeStruct(total.shape, F32),
        ),
        (6 * piece * tall * tall * width, 8 * gated.size),
        (gated, factor, factor_turned, square, cross, pull, cotangent, total),
        [
            pl.BlockSpec((ctx, count, rows, width), lambda s: (0, s, 0, 0)),
            whole(factor), whole(factor_turned), by_piece, by_piece, by_token, by_token,
            whole(total),
        ],
        after,
        grid=(steps // block,),
        out_specs=(
            pl.BlockSpec((ctx, count, rows, width), lambda s: (0, s, 0, 0)),
            whole(total),
        ),
        input_output_aliases={7: 1},
        name="second",
    )


def gate_body(slab, offset, ctx, carried, moved_ref, signal_ref, slope_ref, *refs):
    first_ref, gate_ref, sum_ref, turn, total_ref = refs[carried:]
    rows, depth, width = signal_ref.shape
    count = moved_ref.shape[0]
    piece = count // ctx

    @pl.when(pl.program_id(0) == 0)
    def _():
        total_ref[...] = jnp.zeros_like(total_ref)

    for lane in range(width // 128):
        turn[lane] = (
            moved_ref[:, :, lane * 128 : (lane + 1) * 128]
            .astype(F32)
            .reshape(count * rows, 128)
        )
    total = total_ref[...]
    for a in range(rows):
        grad = jnp.concatenate(
            [turn[lane, pl.ds(a, count, stride=rows), :] for lane in range(width // 128)], axis=1
        )
        own = jnp.concatenate(
            [signal_ref[a, d * slab + offset : d * slab + offset + piece, :] for d in range(ctx)],
            axis=0,
        )
        first = (grad * sigmoid(own.astype(F32))).astype(BF16)
        first_ref[a] = first
        gate_ref[a] = (grad * slope_ref[a].astype(F32)).astype(BF16)
        total += dot(signal_ref[a], first, 1, 1)
    total_ref[...] = total

    @pl.when(pl.program_id(0) == pl.num_programs(0) - 1)
    def _():
        sum_ref[...] = total_ref[...].astype(BF16).reshape(sum_ref.shape)


def gate(moved, signal, slope, slab, k, pieces, sums, ctx, after=()):
    rows, depth, width = signal.shape
    count = moved.shape[0]
    block = min(16, rows)
    by_row = pl.BlockSpec((block, count, width), lambda s: (s, 0, 0))
    return call(
        functools.partial(gate_body, slab, k * (count // ctx), ctx, len(sums)),
        (
            jax.ShapeDtypeStruct((rows, count, width), BF16),
            jax.ShapeDtypeStruct((rows, count, width), BF16),
            jax.ShapeDtypeStruct(sums[0].shape, BF16)
            if sums
            else jax.ShapeDtypeStruct((ctx, pieces * (depth // ctx), count), BF16),
        ),
        (2 * rows * depth * count * width, 2 * rows * width * (depth + 4 * count)),
        (moved, signal, slope, *sums),
        [
            pl.BlockSpec((count, block, width), lambda s: (0, s, 0)),
            pl.BlockSpec((block, depth, width), lambda s: (s, 0, 0)),
            by_row,
            *([pl.BlockSpec(memory_space=pl.ANY)] * len(sums)),
        ],
        after,
        grid=(rows // block,),
        out_specs=(
            by_row,
            by_row,
            pl.BlockSpec((ctx, depth // ctx, count), lambda s: (0, k, 0)),
        ),
        scratch_shapes=[
            pltpu.VMEM((width // 128, count * block, 128), F32),
            pltpu.VMEM((depth, count), F32),
        ],
        input_output_aliases={3: 2} if sums else {},
        name="gate",
    )


def signal_body(offsets, slab, ctx, factor_ref, *refs):
    pieces = len(offsets)
    firsts, gates, out_ref = refs[:pieces], refs[pieces : 2 * pieces], refs[-1]
    for a in range(out_ref.shape[0]):
        grads = jnp.concatenate([first[a] for first in firsts], axis=0)
        total = dot(factor_ref[...], grads, 1, 0)
        for gate_ref, offset in zip(gates, offsets):
            piece = gate_ref.shape[1] // ctx
            for d in range(ctx):
                place = slice(d * slab + offset, d * slab + offset + piece)
                out_ref[a, place, :] = (
                    total[place] + gate_ref[a, d * piece : (d + 1) * piece, :].astype(F32)
                ).astype(BF16)


def signal_grad(factor, firsts, gates, offsets, slab, ctx, after=()):
    rows, _, width = firsts[0].shape
    depth = factor.shape[0]
    block = min(8, rows)
    by_row = [pl.BlockSpec((block, *array.shape[1:]), lambda s: (s, 0, 0)) for array in firsts]
    return call(
        functools.partial(signal_body, offsets, slab, ctx),
        jax.ShapeDtypeStruct((rows, depth, width), BF16),
        (2 * rows * depth * depth * width, 6 * rows * depth * width),
        (factor, *firsts, *gates),
        [whole(factor), *by_row, *by_row],
        after,
        grid=(rows // block,),
        out_specs=pl.BlockSpec((block, depth, width), lambda s: (s, 0, 0)),
        name="signal_grad",
    )


def fold_body(scale, mine_ref, values_ref, got_ref, *refs):
    del mine_ref
    total = values_ref[...].reshape(refs[-1].shape) + got_ref[...].astype(F32)
    refs[-1][...] = total * scale


def fold(values, got, mine, scale, after=()):
    blocks, _, rows, columns = values.shape
    return pl.pallas_call(
        functools.partial(fold_body, scale),
        out_shape=jax.ShapeDtypeStruct((blocks, rows, columns), F32),
        grid_spec=pltpu.PrefetchScalarGridSpec(
            num_scalar_prefetch=1,
            grid=(blocks,),
            in_specs=[
                pl.BlockSpec((1, 1, rows, columns), lambda s, mine: (s, mine[0], 0, 0)),
                pl.BlockSpec((1, rows, columns), lambda s, mine: (s, 0, 0)),
                *([pl.BlockSpec(memory_space=pl.ANY)] * len(after)),
            ],
            out_specs=pl.BlockSpec((1, rows, columns), lambda s, mine: (s, 0, 0)),
        ),
        compiler_params=pltpu.CompilerParams(vmem_limit_bytes=56 * MIB),
        cost_estimate=pl.CostEstimate(
            flops=got.size, bytes_accessed=10 * got.size, transcendentals=0
        ),
        name="fold",
    )(mine.reshape(1), values, got, *after)


def finish_body(scale, mine_ref, values_ref, got_ref, *refs):
    del mine_ref
    up_ref, down_ref, gain_ref = refs[-3:]
    total = (values_ref[0, 0] + got_ref[0].astype(F32)) * scale
    rows, width = up_ref.shape[0], total.shape[1]
    start = 0
    for lane in range(0, up_ref.shape[1], width):
        up_ref[:, lane : lane + width] = total[start : start + rows]
        start += rows
    down_ref[...] = total[start : start + down_ref.shape[0]]
    start += down_ref.shape[0]
    gain_ref[...] = total[start : start + 1, : gain_ref.shape[1]]


def finish_weights(values, got, mine, shapes, scale, after):
    _, _, rows, columns = values.shape
    return pl.pallas_call(
        functools.partial(finish_body, scale),
        out_shape=tuple(jax.ShapeDtypeStruct(shape, F32) for shape in shapes),
        grid_spec=pltpu.PrefetchScalarGridSpec(
            num_scalar_prefetch=1,
            grid=(1,),
            in_specs=[
                pl.BlockSpec((1, 1, rows, columns), lambda s, mine: (0, mine[0], 0, 0)),
                pl.BlockSpec((1, rows, columns), lambda s, mine: (0, 0, 0)),
                *([pl.BlockSpec(memory_space=pl.ANY)] * len(after)),
            ],
            out_specs=tuple(pl.BlockSpec(shape, lambda s, mine: (0, 0)) for shape in shapes),
        ),
        compiler_params=pltpu.CompilerParams(vmem_limit_bytes=56 * MIB),
        cost_estimate=pl.CostEstimate(
            flops=got.size, bytes_accessed=10 * got.size, transcendentals=0
        ),
        name="finish_weights",
    )(mine.reshape(1), values, got, *after)


class Halving:
    def __init__(self, values, ctx, scale):
        self.ctx, self.bit, self.scale = ctx, 1, scale
        self.values = values
        self.halve()

    def halve(self):
        self.halves = self.values.reshape((-1, 2) + self.values.shape[1:])
        self.mine = (lax.axis_index("ctx") // self.bit) % 2
        self.give = lax.dynamic_index_in_dim(
            self.halves, 1 - self.mine, 1, keepdims=False
        ).astype(BF16)

    def send(self):
        bit = self.bit
        self.got = lax.ppermute(self.give, "ctx", [(i, i ^ bit) for i in range(self.ctx)])
        return self.got

    def keep(self, after=()):
        self.bit = 2 * self.bit
        scale = 1.0 if self.bit < self.ctx else self.scale
        self.values = fold(self.halves, self.got, self.mine, scale, after)
        if self.bit < self.ctx:
            self.halve()

    def finish(self, after=()):
        while self.bit < self.ctx:
            self.send()
            self.keep(after)
        return self.values[0]


def block_total_body(pieces, ctx, scale, parts_ref, first_ref, *rest):
    rows = first_ref.shape[0]
    count = parts_ref.shape[2]
    size = count // ctx

    def total_of(start, stop):
        total = parts_ref[0, start:stop].astype(F32)
        for source in range(1, ctx):
            total += parts_ref[source, start:stop].astype(F32)
        return total * scale

    for k in range(pieces):
        total = total_of(k * rows, (k + 1) * rows)
        for d in range(ctx):
            place = (d * pieces + k) * size
            first_ref[:, place : place + size] = total[:, d * size : (d + 1) * size]
    if rest:
        rest[0][...] = total_of(pieces * rows, parts_ref.shape[1])


def block_total(parts, pieces, ctx, scale, after=()):
    _, all_rows, count = parts.shape
    depth = pieces * count
    more = all_rows - pieces * (depth // ctx)
    shapes = [jax.ShapeDtypeStruct((depth // ctx, depth), F32)]
    if more:
        shapes.append(jax.ShapeDtypeStruct((more, count), F32))
    return call(
        functools.partial(block_total_body, pieces, ctx, scale),
        tuple(shapes),
        (parts.size, 4 * parts.size),
        (parts,),
        [whole(parts)],
        after,
        grid=(1,),
        out_specs=tuple(pl.BlockSpec(shape.shape, lambda s: (0, 0)) for shape in shapes),
        name="block_total",
    )


def hold(array, after):
    return pl.pallas_call(
        lambda *refs: None,
        out_shape=jax.ShapeDtypeStruct(array.shape, array.dtype),
        in_specs=[pl.BlockSpec(memory_space=pl.ANY)] * (1 + len(after)),
        out_specs=pl.BlockSpec(memory_space=pl.ANY),
        input_output_aliases={0: 0},
        compiler_params=pltpu.CompilerParams(vmem_limit_bytes=56 * MIB),
        name="hold",
    )(array, *after)


def from_groups(partial_value):
    return lax.all_gather(partial_value, "ch")


def exchange(block):
    return lax.all_to_all(block, "ctx", split_axis=0, concat_axis=0, tiled=True)


def shards(ctx, channels, token_count, signal, factor_first, factor_second, up_weight,
           down_weight, norm_gain, cotangent):
    rows, depth, width = signal.shape
    slab, tall, _ = cotangent.shape
    first, factor = factor_first[0], factor_second[0]
    up, down = up_weight[0], down_weight[0]
    hidden = up.shape[1]
    factor_turned, up_turned, down_turned = factor.T, up.T, down.T
    pieces = 2 if slab % 32 == 0 else 1
    size = slab // pieces
    unit = min(16, size)
    inner = 2
    by_owner = first.reshape(depth, ctx, pieces, size)
    columns = [by_owner[:, :, k].reshape(depth, ctx * size) for k in range(pieces)]
    sums = (
        jnp.zeros((width, hidden), F32),
        jnp.zeros((width, hidden), F32),
        jnp.zeros((1, width), F32),
    )
    layer_pull = ()
    second_sum = jnp.zeros((tall, tall), F32)
    slopes, arrived, moved = [], [], []
    for k in range(pieces):
        gated, slope = first_mix(signal, columns[k].T, slab, k * size, ctx)
        slopes.append(slope)
        arrived.append(exchange(gated).reshape(ctx, size, rows, width))
    waits = ()
    scale = token_count ** (-0.5)
    gain_width = width // ctx
    for k in range(pieces):
        square = from_groups(squares(arrived[k], factor_turned, inner, waits))
        crosses = []
        for begin in range(0, size, unit):
            layer, pull, cross, *sums = mlp(
                arrived[k], (begin, unit), factor_turned, square, norm_gain, up, up_turned, down,
                down_turned, cotangent, k * size, sums, layer_pull, channels,
            )
            layer_pull = (layer, pull)
            crosses.append(cross)
        cross = from_groups(jnp.concatenate(crosses))
        waits = ()
        if k == pieces - 1:
            up_sum, down_sum, gain_sum = sums
            packed = jnp.concatenate(
                [
                    up_sum.reshape(ctx, gain_width, hidden // width, width)
                    .transpose(0, 2, 1, 3)
                    .reshape(ctx, hidden // ctx, width),
                    down_sum.T.reshape(ctx, hidden // ctx, width),
                    jnp.pad(
                        gain_sum.reshape(ctx, 1, gain_width),
                        ((0, 0), (0, 15), (0, width - gain_width)),
                    ),
                ],
                axis=1,
            )
            weights = Halving(packed, ctx, scale)
            waits = (weights.give,)
        back, second_sum = second(
            arrived[k], factor, factor_turned, square, cross, pull, cotangent, k * size,
            second_sum, channels, waits,
        )
        waits = (back,)
        if pieces > 1 and k == pieces - 1:
            back = hold(back, (weights.send(),))
            weights.keep((back,))
        moved.append(exchange(back.reshape(ctx * size, rows, width)))
    count = ctx * size
    own_rows, joint = tall // ctx, count == tall
    sums, firsts, gates, waits = (), [], [], ()
    factor_sorted = jnp.concatenate(columns, axis=1)
    if joint:
        above = ((0, 0), (pieces * (depth // ctx), 0), (0, 0))
        sums = (jnp.pad(second_sum.reshape(ctx, own_rows, tall).astype(BF16), above),)
    for k in range(pieces):
        if k == pieces - 1:
            while 2 * weights.bit < ctx:
                weights.send()
                weights.keep(tuple(firsts))
            waits = (weights.give, factor_sorted)
        first_grad, gate_grad, first_sum = gate(
            moved[k], signal, slopes[k], slab, k, pieces, sums, ctx, waits
        )
        sums = (first_sum,)
        firsts.append(first_grad)
        gates.append(gate_grad)
    last_got = weights.send()
    parts = exchange(hold(first_sum, (last_got,)))
    grad_signal = signal_grad(
        factor_sorted, firsts, gates, tuple(k * size for k in range(pieces)), slab, ctx
    )
    grad_up, grad_down, grad_gain = finish_weights(
        weights.halves, last_got, weights.mine,
        ((gain_width, hidden), (hidden // ctx, width), (1, gain_width)), scale, (grad_signal,),
    )
    grad_first, *rest = block_total(parts, pieces, ctx, scale, (grad_signal, grad_gain))
    grad_second = (
        rest[0] if joint else Halving(second_sum.reshape(ctx, own_rows, tall), ctx, scale).finish()
    )
    return (
        layer,
        grad_signal,
        grad_first[None],
        grad_second[None],
        grad_up[None],
        grad_down[None],
        grad_gain,
    )


def solution(mesh):
    placed = (
        P("ctx", None, "ch"),
        P("ch", None, None),
        P("ch", None, None),
        P("ch", None, None),
        P("ch", None, None),
        P("ch", None),
        P("ctx", None, "ch"),
    )

    def layer(signal, factor_first, factor_second, up_weight, down_weight, norm_gain, cotangent):
        body = functools.partial(
            shards, mesh.shape["ctx"], signal.shape[2], signal.shape[0] * signal.shape[1]
        )
        return jax.shard_map(
            body,
            mesh=mesh,
            in_specs=placed,
            out_specs=(
                P("ctx", None, "ch"),
                P("ctx", None, "ch"),
                P("ch", "ctx", None),
                P("ch", "ctx", None),
                P("ch", "ctx", None),
                P("ch", "ctx", None),
                P("ch", "ctx"),
            ),
            check_vma=False,
        )(signal, factor_first, factor_second, up_weight, down_weight, norm_gain, cotangent)

    return layer
```

```python
import functools

import jax
import jax.numpy as jnp
from jax import lax
from jax.experimental import pallas as pl
from jax.experimental.pallas import tpu as pltpu
from jax.sharding import PartitionSpec as P

EPSILON = 1e-05
TANH_SCALE = 0.7978845608028654
TANH_CUBIC = 0.044715
BF16 = jnp.bfloat16
F32 = jnp.float32
MIB = 1024 * 1024


def sigmoid(values):
    return 0.5 * jnp.tanh(0.5 * values) + 0.5


def dot(left, right, left_dim, right_dim):
    return lax.dot_general(
        left, right, (((left_dim,), (right_dim,)), ((), ())), preferred_element_type=F32
    )


def to_row(column):
    return jnp.broadcast_to(column, (column.shape[0], 128)).T[0:1, :]


def to_column(row, width):
    spread = jnp.broadcast_to(row, (128, row.shape[1])).T
    return jnp.concatenate([spread] * (width // 128), axis=1)


def call(body, out_shape, cost, operands, in_specs, after=(), vmem=56, **options):
    flops, bytes_accessed = cost
    given, waits = len(operands), len(after)

    def ordered(*refs):
        body(*refs[:given], *refs[given + waits :])

    return pl.pallas_call(
        ordered,
        out_shape=out_shape,
        in_specs=[*in_specs, *([pl.BlockSpec(memory_space=pl.ANY)] * waits)],
        compiler_params=pltpu.CompilerParams(vmem_limit_bytes=vmem * MIB),
        cost_estimate=pl.CostEstimate(
            flops=int(flops), bytes_accessed=int(bytes_accessed), transcendentals=0
        ),
        **options,
    )(*operands, *after)


def whole(array):
    return pl.BlockSpec(array.shape, lambda s: (0,) * array.ndim)


def first_mix_body(slab, offset, ctx, signal_ref, factor_ref, gated_ref, slope_ref, turn):
    rows, depth, width = signal_ref.shape
    piece = gated_ref.shape[0] // ctx
    count = ctx * piece
    for a in range(rows):
        first = dot(factor_ref[...], signal_ref[a], 1, 0)
        own = jnp.concatenate(
            [signal_ref[a, d * slab + offset : d * slab + offset + piece, :] for d in range(ctx)],
            axis=0,
        )
        gate = sigmoid(own.astype(F32))
        gated = first * gate
        slope_ref[a] = (gated * (1.0 - gate)).astype(BF16)
        for lane in range(width // 128):
            turn[lane, pl.ds(a, count, stride=rows), :] = gated[:, lane * 128 : (lane + 1) * 128]
    for lane in range(width // 128):
        gated_ref[:, :, lane * 128 : (lane + 1) * 128] = (
            turn[lane].reshape(count, rows, 128).astype(BF16)
        )


def first_mix(signal, factor_turned, slab, offset, ctx, after=()):
    rows, depth, width = signal.shape
    count = factor_turned.shape[0]
    block = min(16, rows)
    return call(
        functools.partial(first_mix_body, slab, offset, ctx),
        (
            jax.ShapeDtypeStruct((count, rows, width), BF16),
            jax.ShapeDtypeStruct((rows, count, width), BF16),
        ),
        (2 * rows * depth * count * width, 2 * rows * width * (depth + 2 * count)),
        (signal, factor_turned),
        [
            pl.BlockSpec((block, depth, width), lambda s: (s, 0, 0)),
            pl.BlockSpec((count, depth), lambda s: (0, 0)),
        ],
        after,
        grid=(rows // block,),
        out_specs=(
            pl.BlockSpec((count, block, width), lambda s: (0, s, 0)),
            pl.BlockSpec((block, count, width), lambda s: (s, 0, 0)),
        ),
        scratch_shapes=[pltpu.VMEM((width // 128, count * block, 128), F32)],
        name="first_mix",
    )


def tokens_of(gated_ref, t):
    ctx, _, rows, width = gated_ref.shape
    return gated_ref[:, t].reshape(ctx * rows, width)


def square_body(gated_ref, factor_ref, square_ref):
    steps, inner, _ = square_ref.shape
    for t in range(steps * inner):
        mixed = dot(factor_ref[...], tokens_of(gated_ref, t), 1, 0)
        square_ref[t // inner, t % inner : t % inner + 1, :] = to_row(
            jnp.sum(mixed * mixed, axis=1, keepdims=True)
        )


def squares(gated, factor_turned, inner, after=()):
    ctx, piece, rows, width = gated.shape
    tall = factor_turned.shape[0]
    block = min(8, piece)
    return call(
        square_body,
        jax.ShapeDtypeStruct((piece // inner, inner, tall), F32),
        (2 * piece * tall * tall * width, 2 * gated.size),
        (gated, factor_turned),
        [
            pl.BlockSpec((ctx, block, rows, width), lambda s: (0, s, 0, 0)),
            whole(factor_turned),
        ],
        after,
        grid=(piece // block,),
        out_specs=pl.BlockSpec((block // inner, inner, tall), lambda s: (s, 0, 0)),
        name="squares",
    )


def gathered(parts_ref, step, t):
    return sum(parts_ref[g, step, t : t + 1, :] for g in range(parts_ref.shape[0]))


def inverse_of(square_ref, step, t, channels):
    return lax.rsqrt(gathered(square_ref, step, t) * (1.0 / channels) + EPSILON)


def mlp_body(
    channels, carried, gated_ref, factor_ref, square_ref, gain_ref, up_ref, up_turned_ref,
    down_ref, down_turned_ref, cotangent_ref, up_in_ref, down_in_ref, gain_in_ref, *refs,
):
    (layer_ref, pull_ref, cross_ref, up_out_ref, down_out_ref, gain_out_ref,
     mixed_all, normed_all, act_all, pre_all, spread_all) = refs[carried:]
    inner = square_ref.shape[2]
    tall = factor_ref.shape[0]
    width = gain_ref.shape[1]
    hidden = up_ref.shape[1]

    @pl.when(pl.program_id(0) == 0)
    def _():
        up_out_ref[...] = up_in_ref[...]
        down_out_ref[...] = down_in_ref[...]
        gain_out_ref[...] = gain_in_ref[...]

    for t in range(inner):
        inverse = inverse_of(square_ref, 0, t, channels)
        part = slice(t * tall, (t + 1) * tall)
        mixed = dot(factor_ref[...], tokens_of(gated_ref, t), 1, 0)
        spread = to_column(inverse, width)
        mixed_all[part, :] = mixed
        spread_all[part, :] = spread
        normed_all[part, :] = (mixed * spread * gain_ref[...]).astype(BF16)
    upstream = cotangent_ref[...].reshape(inner * tall, width)
    normed = normed_all[...]
    step = min(256, hidden)
    for h in range(0, hidden, step):
        part = slice(h, h + step)
        pre = dot(normed, up_ref[:, part], 1, 0)
        back = dot(upstream, down_turned_ref[:, part], 1, 0)
        square = pre * pre
        lean = jnp.tanh(pre * (square * (TANH_SCALE * TANH_CUBIC) + TANH_SCALE))
        half = 0.5 * lean + 0.5
        act = pre * half
        act_all[:, part] = act.astype(BF16)
        bend = square * (6.0 * TANH_SCALE * TANH_CUBIC) + 2.0 * TANH_SCALE
        pre_all[:, part] = (back * (half + act * (1.0 - half) * bend)).astype(BF16)
    mixed = mixed_all[...]
    layer = mixed + dot(act_all[...], down_ref[...], 1, 0)
    layer_ref[...] = layer.astype(BF16).reshape(layer_ref.shape)
    down_out_ref[...] += dot(upstream, act_all[...], 0, 0)
    up_out_ref[...] += dot(normed, pre_all[...], 0, 0)
    grad_normed = dot(pre_all[...], up_turned_ref[...], 1, 0)
    spread = spread_all[...]
    gain = gain_ref[...]
    weighed = grad_normed * mixed
    gain_out_ref[...] += jnp.sum(weighed * spread, axis=0, keepdims=True)
    cross = jnp.sum(weighed * gain, axis=1, keepdims=True)
    for t in range(inner):
        cross_ref[0, t : t + 1, :] = to_row(cross[t * tall : (t + 1) * tall])
    pull_ref[...] = (grad_normed * gain * spread).astype(BF16).reshape(pull_ref.shape)


def mlp(gated, part, factor_turned, square, gain, up, up_turned, down, down_turned, cotangent,
        first_piece, sums, layer_pull, channels, after=()):
    ctx, _, rows, width = gated.shape
    groups, _, inner, tall = square.shape
    hidden = up.shape[1]
    begin, piece = part
    steps, skip = piece // inner, begin // inner
    start = (first_piece + begin) // inner
    tokens = inner * tall
    by_token = pl.BlockSpec((inner, tall, width), lambda s: (s + start, 0, 0))
    stays = pl.BlockSpec(memory_space=pl.ANY)
    full = jax.ShapeDtypeStruct(cotangent.shape, BF16)
    carried = len(layer_pull)
    aliases = {9: 3, 10: 4, 11: 5}
    for i in range(carried):
        aliases[12 + i] = i
    return call(
        functools.partial(mlp_body, channels, carried),
        (
            full,
            full,
            jax.ShapeDtypeStruct((steps, inner, tall), F32),
            *(jax.ShapeDtypeStruct(array.shape, F32) for array in sums),
        ),
        (12 * piece * tall * width * hidden, 8 * piece * tall * width),
        (gated, factor_turned, square, gain, up, up_turned, down, down_turned, cotangent, *sums,
         *layer_pull),
        [
            pl.BlockSpec((ctx, inner, rows, width), lambda s: (0, s + skip, 0, 0)),
            whole(factor_turned),
            pl.BlockSpec((groups, 1, inner, tall), lambda s: (0, s + skip, 0, 0)),
            whole(gain), whole(up), whole(up_turned), whole(down), whole(down_turned),
            by_token,
            *(whole(array) for array in sums),
            *([stays] * carried),
        ],
        after,
        grid=(steps,),
        out_specs=(
            by_token, by_token,
            pl.BlockSpec((1, inner, tall), lambda s: (s, 0, 0)),
            *(whole(array) for array in sums),
        ),
        scratch_shapes=[
            pltpu.VMEM((tokens, width), F32),
            pltpu.VMEM((tokens, width), BF16),
            pltpu.VMEM((tokens, hidden), BF16),
            pltpu.VMEM((tokens, hidden), BF16),
            pltpu.VMEM((tokens, width), F32),
        ],
        input_output_aliases=aliases,
        name="mlp",
    )


def second_body(
    channels, gated_ref, factor_ref, factor_turned_ref, square_ref, cross_ref, pull_ref,
    cotangent_ref, sum_in_ref, moved_ref, sum_out_ref,
):
    _, steps, inner, tall = square_ref.shape
    ctx, _, rows, width = gated_ref.shape

    @pl.when(pl.program_id(0) == 0)
    def _():
        sum_out_ref[...] = sum_in_ref[...]

    total = sum_out_ref[...]
    for t in range(steps * inner):
        gated = tokens_of(gated_ref, t)
        mixed = dot(factor_turned_ref[...], gated, 1, 0)
        inverse = inverse_of(square_ref, t // inner, t % inner, channels)
        cross = gathered(cross_ref, t // inner, t % inner)
        weight = to_column(inverse * inverse * inverse * cross * (1.0 / channels), width)
        grad = (
            cotangent_ref[t].astype(F32) + pull_ref[t].astype(F32) - mixed * weight
        ).astype(BF16)
        total += dot(gated, grad, 1, 1)
        moved_ref[:, t] = dot(factor_ref[...], grad, 1, 0).astype(BF16).reshape(ctx, rows, width)
    sum_out_ref[...] = total


def second(gated, factor, factor_turned, square, cross, pull, cotangent, first_piece, total,
           channels, after=()):
    ctx, piece, rows, width = gated.shape
    groups, steps, inner, tall = square.shape
    block = max(size for size in (4, 2, 1) if steps % size == 0)
    count = block * inner
    start = first_piece // count
    by_piece = pl.BlockSpec((groups, block, inner, tall), lambda s: (0, s, 0, 0))
    by_token = pl.BlockSpec((count, tall, width), lambda s: (s + start, 0, 0))
    return call(
        functools.partial(second_body, channels),
        (
            jax.ShapeDtypeStruct(gated.shape, BF16),
            jax.ShapeDtypeStruct(total.shape, F32),
        ),
        (6 * piece * tall * tall * width, 8 * gated.size),
        (gated, factor, factor_turned, square, cross, pull, cotangent, total),
        [
            pl.BlockSpec((ctx, count, rows, width), lambda s: (0, s, 0, 0)),
            whole(factor), whole(factor_turned), by_piece, by_piece, by_token, by_token,
            whole(total),
        ],
        after,
        grid=(steps // block,),
        out_specs=(
            pl.BlockSpec((ctx, count, rows, width), lambda s: (0, s, 0, 0)),
            whole(total),
        ),
        input_output_aliases={7: 1},
        name="second",
    )


def gate_body(slab, offset, ctx, carried, moved_ref, signal_ref, slope_ref, *refs):
    first_ref, gate_ref, sum_ref, turn, total_ref = refs[carried:]
    rows, depth, width = signal_ref.shape
    count = moved_ref.shape[0]
    piece = count // ctx

    @pl.when(pl.program_id(0) == 0)
    def _():
        total_ref[...] = jnp.zeros_like(total_ref)

    for lane in range(width // 128):
        turn[lane] = (
            moved_ref[:, :, lane * 128 : (lane + 1) * 128]
            .astype(F32)
            .reshape(count * rows, 128)
        )
    total = total_ref[...]
    for a in range(rows):
        grad = jnp.concatenate(
            [turn[lane, pl.ds(a, count, stride=rows), :] for lane in range(width // 128)], axis=1
        )
        own = jnp.concatenate(
            [signal_ref[a, d * slab + offset : d * slab + offset + piece, :] for d in range(ctx)],
            axis=0,
        )
        first = (grad * sigmoid(own.astype(F32))).astype(BF16)
        first_ref[a] = first
        gate_ref[a] = (grad * slope_ref[a].astype(F32)).astype(BF16)
        total += dot(signal_ref[a], first, 1, 1)
    total_ref[...] = total

    @pl.when(pl.program_id(0) == pl.num_programs(0) - 1)
    def _():
        sum_ref[...] = total_ref[...].astype(BF16).reshape(sum_ref.shape)


def gate(moved, signal, slope, slab, k, pieces, sums, ctx, after=()):
    rows, depth, width = signal.shape
    count = moved.shape[0]
    block = min(16, rows)
    by_row = pl.BlockSpec((block, count, width), lambda s: (s, 0, 0))
    return call(
        functools.partial(gate_body, slab, k * (count // ctx), ctx, len(sums)),
        (
            jax.ShapeDtypeStruct((rows, count, width), BF16),
            jax.ShapeDtypeStruct((rows, count, width), BF16),
            jax.ShapeDtypeStruct(sums[0].shape, BF16)
            if sums
            else jax.ShapeDtypeStruct((ctx, pieces * (depth // ctx), count), BF16),
        ),
        (2 * rows * depth * count * width, 2 * rows * width * (depth + 4 * count)),
        (moved, signal, slope, *sums),
        [
            pl.BlockSpec((count, block, width), lambda s: (0, s, 0)),
            pl.BlockSpec((block, depth, width), lambda s: (s, 0, 0)),
            by_row,
            *([pl.BlockSpec(memory_space=pl.ANY)] * len(sums)),
        ],
        after,
        grid=(rows // block,),
        out_specs=(
            by_row,
            by_row,
            pl.BlockSpec((ctx, depth // ctx, count), lambda s: (0, k, 0)),
        ),
        scratch_shapes=[
            pltpu.VMEM((width // 128, count * block, 128), F32),
            pltpu.VMEM((depth, count), F32),
        ],
        input_output_aliases={3: 2} if sums else {},
        name="gate",
    )


def signal_body(offsets, slab, ctx, factor_ref, *refs):
    pieces = len(offsets)
    firsts, gates, out_ref = refs[:pieces], refs[pieces : 2 * pieces], refs[-1]
    for a in range(out_ref.shape[0]):
        grads = jnp.concatenate([first[a] for first in firsts], axis=0)
        total = dot(factor_ref[...], grads, 1, 0)
        for gate_ref, offset in zip(gates, offsets):
            piece = gate_ref.shape[1] // ctx
            for d in range(ctx):
                place = slice(d * slab + offset, d * slab + offset + piece)
                out_ref[a, place, :] = (
                    total[place] + gate_ref[a, d * piece : (d + 1) * piece, :].astype(F32)
                ).astype(BF16)


def signal_grad(factor, firsts, gates, offsets, slab, ctx, after=()):
    rows, _, width = firsts[0].shape
    depth = factor.shape[0]
    block = min(8, rows)
    by_row = [pl.BlockSpec((block, *array.shape[1:]), lambda s: (s, 0, 0)) for array in firsts]
    return call(
        functools.partial(signal_body, offsets, slab, ctx),
        jax.ShapeDtypeStruct((rows, depth, width), BF16),
        (2 * rows * depth * depth * width, 6 * rows * depth * width),
        (factor, *firsts, *gates),
        [whole(factor), *by_row, *by_row],
        after,
        grid=(rows // block,),
        out_specs=pl.BlockSpec((block, depth, width), lambda s: (s, 0, 0)),
        name="signal_grad",
    )


def fold_body(scale, mine_ref, values_ref, got_ref, *refs):
    del mine_ref
    total = values_ref[...].reshape(refs[-1].shape) + got_ref[...].astype(F32)
    refs[-1][...] = total * scale


def fold(values, got, mine, scale, after=()):
    blocks, _, rows, columns = values.shape
    return pl.pallas_call(
        functools.partial(fold_body, scale),
        out_shape=jax.ShapeDtypeStruct((blocks, rows, columns), F32),
        grid_spec=pltpu.PrefetchScalarGridSpec(
            num_scalar_prefetch=1,
            grid=(blocks,),
            in_specs=[
                pl.BlockSpec((1, 1, rows, columns), lambda s, mine: (s, mine[0], 0, 0)),
                pl.BlockSpec((1, rows, columns), lambda s, mine: (s, 0, 0)),
                *([pl.BlockSpec(memory_space=pl.ANY)] * len(after)),
            ],
            out_specs=pl.BlockSpec((1, rows, columns), lambda s, mine: (s, 0, 0)),
        ),
        compiler_params=pltpu.CompilerParams(vmem_limit_bytes=56 * MIB),
        cost_estimate=pl.CostEstimate(
            flops=got.size, bytes_accessed=10 * got.size, transcendentals=0
        ),
        name="fold",
    )(mine.reshape(1), values, got, *after)


def finish_body(scale, mine_ref, values_ref, got_ref, *refs):
    del mine_ref
    up_ref, down_ref, gain_ref = refs[-3:]
    total = (values_ref[0, 0] + got_ref[0].astype(F32)) * scale
    rows, width = up_ref.shape[0], total.shape[1]
    start = 0
    for lane in range(0, up_ref.shape[1], width):
        up_ref[:, lane : lane + width] = total[start : start + rows]
        start += rows
    down_ref[...] = total[start : start + down_ref.shape[0]]
    start += down_ref.shape[0]
    gain_ref[...] = total[start : start + 1, : gain_ref.shape[1]]


def finish_weights(values, got, mine, shapes, scale, after):
    _, _, rows, columns = values.shape
    return pl.pallas_call(
        functools.partial(finish_body, scale),
        out_shape=tuple(jax.ShapeDtypeStruct(shape, F32) for shape in shapes),
        grid_spec=pltpu.PrefetchScalarGridSpec(
            num_scalar_prefetch=1,
            grid=(1,),
            in_specs=[
                pl.BlockSpec((1, 1, rows, columns), lambda s, mine: (0, mine[0], 0, 0)),
                pl.BlockSpec((1, rows, columns), lambda s, mine: (0, 0, 0)),
                *([pl.BlockSpec(memory_space=pl.ANY)] * len(after)),
            ],
            out_specs=tuple(pl.BlockSpec(shape, lambda s, mine: (0, 0)) for shape in shapes),
        ),
        compiler_params=pltpu.CompilerParams(vmem_limit_bytes=56 * MIB),
        cost_estimate=pl.CostEstimate(
            flops=got.size, bytes_accessed=10 * got.size, transcendentals=0
        ),
        name="finish_weights",
    )(mine.reshape(1), values, got, *after)


class Halving:
    def __init__(self, values, ctx, scale):
        self.ctx, self.bit, self.scale = ctx, 1, scale
        self.values = values
        if ctx >= 4:
            quarters = values.reshape((ctx // 4, 2, 2) + values.shape[1:])
            self.values = jnp.swapaxes(quarters, 1, 2).reshape(values.shape)
        self.halve()

    def away(self):
        return {1: 2, 2: 1}.get(self.bit, self.bit) if self.ctx >= 4 else self.bit

    def halve(self):
        self.halves = self.values.reshape((-1, 2) + self.values.shape[1:])
        self.mine = (lax.axis_index("ctx") // self.away()) % 2
        self.give = lax.dynamic_index_in_dim(
            self.halves, 1 - self.mine, 1, keepdims=False
        ).astype(BF16)

    def send(self):
        bit = self.away()
        self.got = lax.ppermute(self.give, "ctx", [(i, i ^ bit) for i in range(self.ctx)])
        return self.got

    def keep(self, after=()):
        self.bit = 2 * self.bit
        scale = 1.0 if self.bit < self.ctx else self.scale
        self.values = fold(self.halves, self.got, self.mine, scale, after)
        if self.bit < self.ctx:
            self.halve()

    def finish(self, after=()):
        while self.bit < self.ctx:
            self.send()
            self.keep(after)
        return self.values[0]


def block_total_body(pieces, ctx, scale, parts_ref, first_ref, *rest):
    rows = first_ref.shape[0]
    count = parts_ref.shape[2]
    size = count // ctx

    def total_of(start, stop):
        total = parts_ref[0, start:stop].astype(F32)
        for source in range(1, ctx):
            total += parts_ref[source, start:stop].astype(F32)
        return total * scale

    for k in range(pieces):
        total = total_of(k * rows, (k + 1) * rows)
        for d in range(ctx):
            place = (d * pieces + k) * size
            first_ref[:, place : place + size] = total[:, d * size : (d + 1) * size]
    if rest:
        rest[0][...] = total_of(pieces * rows, parts_ref.shape[1])


def block_total(parts, pieces, ctx, scale, after=()):
    _, all_rows, count = parts.shape
    depth = pieces * count
    more = all_rows - pieces * (depth // ctx)
    shapes = [jax.ShapeDtypeStruct((depth // ctx, depth), F32)]
    if more:
        shapes.append(jax.ShapeDtypeStruct((more, count), F32))
    return call(
        functools.partial(block_total_body, pieces, ctx, scale),
        tuple(shapes),
        (parts.size, 4 * parts.size),
        (parts,),
        [whole(parts)],
        after,
        grid=(1,),
        out_specs=tuple(pl.BlockSpec(shape.shape, lambda s: (0, 0)) for shape in shapes),
        name="block_total",
    )


def hold(array, after):
    return pl.pallas_call(
        lambda *refs: None,
        out_shape=jax.ShapeDtypeStruct(array.shape, array.dtype),
        in_specs=[pl.BlockSpec(memory_space=pl.ANY)] * (1 + len(after)),
        out_specs=pl.BlockSpec(memory_space=pl.ANY),
        input_output_aliases={0: 0},
        compiler_params=pltpu.CompilerParams(vmem_limit_bytes=56 * MIB),
        name="hold",
    )(array, *after)


def from_groups(partial_value):
    return lax.all_gather(partial_value, "ch")


def exchange(block):
    return lax.all_to_all(block, "ctx", split_axis=0, concat_axis=0, tiled=True)


def shards(ctx, channels, token_count, signal, factor_first, factor_second, up_weight,
           down_weight, norm_gain, cotangent):
    rows, depth, width = signal.shape
    slab, tall, _ = cotangent.shape
    first, factor = factor_first[0], factor_second[0]
    up, down = up_weight[0], down_weight[0]
    hidden = up.shape[1]
    factor_turned, up_turned, down_turned = factor.T, up.T, down.T
    pieces = 2 if slab % 32 == 0 else 1
    size = slab // pieces
    unit = min(16, size)
    inner = 2
    by_owner = first.reshape(depth, ctx, pieces, size)
    columns = [by_owner[:, :, k].reshape(depth, ctx * size) for k in range(pieces)]
    sums = (
        jnp.zeros((width, hidden), F32),
        jnp.zeros((width, hidden), F32),
        jnp.zeros((1, width), F32),
    )
    layer_pull = ()
    second_sum = jnp.zeros((tall, tall), F32)
    slopes, arrived, moved = [], [], []
    for k in range(pieces):
        gated, slope = first_mix(signal, columns[k].T, slab, k * size, ctx)
        slopes.append(slope)
        arrived.append(exchange(gated).reshape(ctx, size, rows, width))
    waits = ()
    scale = token_count ** (-0.5)
    gain_width = width // ctx
    for k in range(pieces):
        square = from_groups(squares(arrived[k], factor_turned, inner, waits))
        crosses = []
        for begin in range(0, size, unit):
            layer, pull, cross, *sums = mlp(
                arrived[k], (begin, unit), factor_turned, square, norm_gain, up, up_turned, down,
                down_turned, cotangent, k * size, sums, layer_pull, channels,
            )
            layer_pull = (layer, pull)
            crosses.append(cross)
        cross = from_groups(jnp.concatenate(crosses))
        waits = ()
        if k == pieces - 1:
            up_sum, down_sum, gain_sum = sums
            packed = jnp.concatenate(
                [
                    up_sum.reshape(ctx, gain_width, hidden // width, width)
                    .transpose(0, 2, 1, 3)
                    .reshape(ctx, hidden // ctx, width),
                    down_sum.T.reshape(ctx, hidden // ctx, width),
                    jnp.pad(
                        gain_sum.reshape(ctx, 1, gain_width),
                        ((0, 0), (0, 15), (0, width - gain_width)),
                    ),
                ],
                axis=1,
            )
            weights = Halving(packed, ctx, scale)
            waits = (weights.give,)
        back, second_sum = second(
            arrived[k], factor, factor_turned, square, cross, pull, cotangent, k * size,
            second_sum, channels, waits,
        )
        waits = (back,)
        if pieces > 1 and k == pieces - 1:
            back = hold(back, (weights.send(),))
            weights.keep((back,))
        moved.append(exchange(back.reshape(ctx * size, rows, width)))
    count = ctx * size
    own_rows, joint = tall // ctx, count == tall
    sums, firsts, gates, waits = (), [], [], ()
    factor_sorted = jnp.concatenate(columns, axis=1)
    if joint:
        above = ((0, 0), (pieces * (depth // ctx), 0), (0, 0))
        sums = (jnp.pad(second_sum.reshape(ctx, own_rows, tall).astype(BF16), above),)
    for k in range(pieces):
        if k == pieces - 1:
            while 2 * weights.bit < ctx:
                weights.send()
                weights.keep(tuple(firsts))
            waits = (weights.give, factor_sorted)
        first_grad, gate_grad, first_sum = gate(
            moved[k], signal, slopes[k], slab, k, pieces, sums, ctx, waits
        )
        sums = (first_sum,)
        firsts.append(first_grad)
        gates.append(gate_grad)
    last_got = weights.send()
    parts = exchange(hold(first_sum, (last_got,)))
    grad_signal = signal_grad(
        factor_sorted, firsts, gates, tuple(k * size for k in range(pieces)), slab, ctx
    )
    grad_up, grad_down, grad_gain = finish_weights(
        weights.halves, last_got, weights.mine,
        ((gain_width, hidden), (hidden // ctx, width), (1, gain_width)), scale, (grad_signal,),
    )
    grad_first, *rest = block_total(parts, pieces, ctx, scale, (grad_signal, grad_gain))
    grad_second = (
        rest[0] if joint else Halving(second_sum.reshape(ctx, own_rows, tall), ctx, scale).finish()
    )
    return (
        layer,
        grad_signal,
        grad_first[None],
        grad_second[None],
        grad_up[None],
        grad_down[None],
        grad_gain,
    )


def solution(mesh):
    placed = (
        P("ctx", None, "ch"),
        P("ch", None, None),
        P("ch", None, None),
        P("ch", None, None),
        P("ch", None, None),
        P("ch", None),
        P("ctx", None, "ch"),
    )

    def layer(signal, factor_first, factor_second, up_weight, down_weight, norm_gain, cotangent):
        body = functools.partial(
            shards, mesh.shape["ctx"], signal.shape[2], signal.shape[0] * signal.shape[1]
        )
        return jax.shard_map(
            body,
            mesh=mesh,
            in_specs=placed,
            out_specs=(
                P("ctx", None, "ch"),
                P("ctx", None, "ch"),
                P("ch", "ctx", None),
                P("ch", "ctx", None),
                P("ch", "ctx", None),
                P("ch", "ctx", None),
                P("ch", "ctx"),
            ),
            check_vma=False,
        )(signal, factor_first, factor_second, up_weight, down_weight, norm_gain, cotangent)

    return layer
```
